256 devices in a mesh: stream: 32 (over x, y, core), normal: 8 (over z).
Axes of the slice: x: 4, y: 4, z: 8, core: 2. Of those that a mesh axis runs over, the one named last changes fastest.
Arguments:
- state: float32 [5, 128, 128, 128], P(None, 'stream', 'normal'), may hold values from -2 to 6.5, as said below
- viscosity: float32 [128, 128, 128], P('stream', 'normal'), may hold values from 200 to 1600
- residual_other: float32 [5, 128, 128, 128], P(None, 'stream', 'normal'), may hold values from -2402 to 2402
Outputs:
- increment: float32 [5, 128, 128, 128], P(None, 'stream', 'normal')
The draws below stay inside these ranges and needn't reach their ends.
Inputs may be any that keep to these rules, and one draw needn't show every extreme that they name: `state`: the conserved variables of a gas with gamma 1.4: density between 0.5 and 2, pressure between 0.5 and 2, streamwise speed at most 1 and the other speeds at most 0.5 in magnitude.
All inputs are finite; a program needn't handle non-finite values.
Results may differ from the reference program's by a relative error of at most 0.0003.
Values sent between devices are 32-bit elements; how exact they have to be, the bound alone decides.
A program may use at most 128 MiB of HBM per device.

```python
import math
import jax
import jax.numpy as jnp
from jax import lax

NX = 128
NY = 128
NZ = 128


def draw_state(key, part):
    keys = jax.random.split(key, 5)
    shape = (NX, NY, NZ)
    rho = jnp.exp(jax.random.uniform(keys[0], shape, jnp.float32, math.log(0.5), math.log(2.0)))
    speed_u = jax.random.uniform(keys[1], shape, jnp.float32, -1.0, 1.0)
    speed_v = jax.random.uniform(keys[2], shape, jnp.float32, -0.5, 0.5)
    speed_w = jax.random.uniform(keys[3], shape, jnp.float32, -0.5, 0.5)
    pressure = jnp.exp(jax.random.uniform(keys[4], shape, jnp.float32, math.log(0.5), math.log(2.0)))
    energy = pressure / 0.4 + 0.5 * rho * (speed_u * speed_u + speed_v * speed_v + speed_w * speed_w)
    return jnp.stack([rho, rho * speed_u, rho * speed_v, rho * speed_w, energy]).astype(jnp.float32)


def draw_viscosity(key, part):
    key = jax.random.fold_in(key, 7)
    keys = jax.random.split(key, 2)
    level = jnp.exp(jax.random.uniform(keys[0], (1, NY, NZ), jnp.float32, math.log(400.0), math.log(1600.0)))
    factor = jnp.exp(jax.random.uniform(keys[1], (NX, NY, NZ), jnp.float32, math.log(0.5), 0.0))
    return (level * factor).astype(jnp.float32)


def draw_residual_other(key, part):
    shape = (5, NX, NY, NZ)
    return (400.0 * jax.random.truncated_normal(key, -6.0, 6.0, shape, jnp.float32)).astype(jnp.float32)


def setup_inputs(seed: int = 0) -> dict:
    splits = jax.random.split(jax.random.key(seed), 4)
    return {
        "state": draw_state(jax.random.fold_in(splits[3], 71), 0),
        "viscosity": draw_viscosity(jax.random.fold_in(splits[3], 71), 0),
        "residual_other": draw_residual_other(jax.random.fold_in(splits[3], 71), 0),
    }


GAMMA = 1.4
GM_ONE = 0.4
STREAM_STEP = 1.0
NORMAL_STEP = 40.0
SMOOTHING = 8.0

def stream_jacobian(state):
    rho, mom_x, mom_y, mom_z, energy = (state[0], state[1], state[2], state[3], state[4])
    speed_u = mom_x / rho
    speed_v = mom_y / rho
    speed_w = mom_z / rho
    square = speed_u * speed_u + speed_v * speed_v + speed_w * speed_w
    pressure = GM_ONE * (energy - 0.5 * rho * square)
    enthalpy = (energy + pressure) / rho
    half = 0.5 * GM_ONE * square
    zero = jnp.zeros_like(speed_u)
    unity = jnp.ones_like(speed_u)
    rows_list = [[zero, unity, zero, zero, zero], [half - speed_u * speed_u, (3.0 - GAMMA) * speed_u, -GM_ONE * speed_v, -GM_ONE * speed_w, GM_ONE * unity], [-speed_u * speed_v, speed_v, speed_u, zero, zero], [-speed_u * speed_w, speed_w, zero, speed_u, zero], [speed_u * (half - enthalpy), enthalpy - GM_ONE * speed_u * speed_u, -GM_ONE * speed_u * speed_v, -GM_ONE * speed_u * speed_w, GAMMA * speed_u]]
    return jnp.stack([jnp.stack(row_items) for row_items in rows_list])

def normal_flux(state):
    rho, mom_x, mom_y, mom_z, energy = (state[0], state[1], state[2], state[3], state[4])
    pressure = GM_ONE * (energy - 0.5 * (mom_x * mom_x + mom_y * mom_y + mom_z * mom_z) / rho)
    speed_v = mom_y / rho
    return jnp.stack([mom_y, mom_x * speed_v, mom_y * speed_v + pressure, mom_z * speed_v, (energy + pressure) * speed_v])

def normal_rhs(state, viscosity, residual_other):
    flux = normal_flux(state)
    both = jnp.concatenate([state, flux], axis=0)
    padded = jnp.pad(both, ((0, 0), (0, 0), (2, 2), (0, 0)))
    count = state.shape[2]

    def planes(shift):
        return padded[:, :, 2 + shift:2 + shift + count]
    qs = {s: planes(s)[:5] for s in (-2, -1, 0, 1, 2)}
    flux_up = planes(1)[5:]
    flux_down = planes(-1)[5:]
    return residual_other - NORMAL_STEP * (flux_up - flux_down) + viscosity[None] * (qs[1] - 2.0 * qs[0] + qs[-1]) - SMOOTHING * (qs[2] - 4.0 * qs[1] + 6.0 * qs[0] - 4.0 * qs[-1] + qs[-2])

def solve_lines(item):
    state_j, sig_j, rhs_j = item
    jac = stream_jacobian(state_j)
    jac_pad = jnp.pad(jac, ((0, 0), (0, 0), (1, 1), (0, 0)))
    eye = jnp.eye(5, dtype=jnp.float32)[:, :, None, None]
    lower_blocks = -STREAM_STEP * jac_pad[:, :, :-2] - sig_j * eye
    upper_blocks = STREAM_STEP * jac_pad[:, :, 2:] - sig_j * eye
    diagonal_blocks = (1.0 + 2.0 * sig_j) * eye
    lower_blocks = jnp.transpose(lower_blocks, (2, 3, 0, 1))
    upper_blocks = jnp.transpose(upper_blocks, (2, 3, 0, 1))
    diagonal_blocks = jnp.transpose(diagonal_blocks, (2, 3, 0, 1))
    source_term = jnp.transpose(rhs_j, (1, 2, 0))
    grid_lines = source_term.shape[1]

    def forward_elimination(carry, step_item):
        e_prev, y_prev = carry
        low, up, dia, rhs_i = step_item
        work = dia - jnp.matmul(low, e_prev, precision=lax.Precision.HIGHEST)
        right = rhs_i - jnp.matmul(low, y_prev[..., None], precision=lax.Precision.HIGHEST)[..., 0]
        sol = jnp.linalg.solve(work, jnp.concatenate([up, right[..., None]], axis=-1))
        e_now = sol[..., :5]
        y_now = sol[..., 5]
        return ((e_now, y_now), (e_now, y_now))
    start_index = (jnp.zeros((grid_lines, 5, 5), jnp.float32), jnp.zeros((grid_lines, 5), jnp.float32))
    unused_slot, (elimination_factor, partial_solution) = lax.scan(forward_elimination, start_index, (lower_blocks, upper_blocks, diagonal_blocks, source_term))

    def backward_substitution(x_next, step_item):
        e_now, y_now = step_item
        x_now = y_now - jnp.matmul(e_now, x_next[..., None], precision=lax.Precision.HIGHEST)[..., 0]
        return (x_now, x_now)
    unused_slot, solution_output = lax.scan(backward_substitution, jnp.zeros((grid_lines, 5), jnp.float32), (elimination_factor, partial_solution), reverse=True)
    return jnp.transpose(solution_output, (2, 0, 1))

def reference(state, viscosity, residual_other):
    rhs = normal_rhs(state, viscosity, residual_other)
    items = (jnp.moveaxis(state, 2, 0), jnp.moveaxis(viscosity, 1, 0), jnp.moveaxis(rhs, 2, 0))
    solved = lax.map(solve_lines, items)
    return jnp.moveaxis(solved, 0, 2)
```

```python
import jax
import jax.numpy as jnp
from jax import lax
from jax.experimental import pallas as pl
from jax.experimental.pallas import tpu as pltpu
from jax.sharding import PartitionSpec as P

N = 32
R = 16
HALF = 64
MESH = pl.DeviceIdType.MESH


def roll_lanes(x):
    return pltpu.roll(x, HALF, axis=x.ndim - 1)


def roll_rows(x, by):
    return pltpu.roll(x, by % 8, axis=x.ndim - 2)


def swap_halves(a, b):
    low = lax.broadcasted_iota(jnp.int32, a.shape, a.ndim - 1) < HALF
    return jnp.where(low, a, roll_lanes(b)), jnp.where(low, roll_lanes(a), b)


def place(shape):
    q = lax.broadcasted_iota(jnp.int32, shape, len(shape) - 2)
    b = lax.broadcasted_iota(jnp.int32, shape, len(shape) - 1) >= HALF
    return q, b


def previous(x, by):
    q, b = place(x.shape)
    if by == 1:
        moved = roll_lanes(jnp.where(b, roll_rows(x, 1), x))
        return jnp.where((q == 0) & ~b, 0.0, moved)
    return jnp.where(q < by // 2, 0.0, roll_rows(x, by // 2))


def following(x, by):
    q, b = place(x.shape)
    if by == 1:
        moved = roll_lanes(jnp.where(b, x, roll_rows(x, -1)))
        return jnp.where((q == 7) & b, 0.0, moved)
    return jnp.where(q >= 8 - by // 2, 0.0, roll_rows(x, -(by // 2)))


def jacobian_rows(u, v, w, h, k):
    return [
        [None, 1.0, None, None, None],
        [0.4 * k - u * u, 1.6 * u, -0.4 * v, -0.4 * w, 0.4],
        [-u * v, v, u, None, None],
        [-u * w, w, None, u, None],
        [u * (0.4 * k - h), h - 0.4 * u * u, -0.4 * u * v, -0.4 * u * w, 1.4 * u],
    ]


def jacobian_times(prm, m):
    u, v, w, h, k = prm
    t = m[1] - u * m[0]
    p = 0.4 * (k * m[0] - u * m[1] - v * m[2] - w * m[3] + m[4])
    return [
        m[1],
        p + u * (m[1] + t),
        v * t + u * m[2],
        w * t + u * m[3],
        u * (p + m[4]) + h * t,
    ]


def row_times_jacobian(g, prm, shift):
    u, v, w, h, k = prm
    e = g[0]
    for value, factor in ((g[1], u), (g[2], v), (g[3], w), (g[4], h)):
        if value is not None:
            e = value * factor if e is None else e + value * factor
    p = g[1] if g[4] is None else g[1] + u * g[4]
    p = 0.4 * p
    s = u + shift

    def part(index, other):
        return other if g[index] is None else s * g[index] + other

    return [
        part(0, k * p - u * e),
        part(1, e - u * p),
        part(2, -(v * p)),
        part(3, -(w * p)),
        part(4, p),
    ]


def scaled(rows, shift, factor):
    out = []
    for r in range(5):
        row = []
        for c in range(5):
            value = rows[r][c]
            if r == c:
                value = shift if value is None else value + shift
            row.append(None if value is None else value * factor)
        out.append(row)
    return out


def plus(a, b):
    if a is None:
        return b
    return a if b is None else a + b


def factor_rows(rows):
    rows = list(rows)
    recip = []
    for p in range(5):
        rec = 1.0 / rows[p][p]
        recip.append(rec)
        for r in range(p + 1, 5):
            weight = rows[r][p] * rec
            tail = rows[r][p + 1 :] - weight[None] * rows[p][p + 1 :] if p < 4 else None
            parts = [rows[r][:p], weight[None], tail] if p else [weight[None], tail]
            rows[r] = jnp.concatenate(parts, axis=0)
    return rows, recip


def solve_rows(lu, recip, right):
    x = list(right)
    for p in range(5):
        for r in range(p + 1, 5):
            x[r] = x[r] - lu[r][p] * x[p]
    for p in range(4, -1, -1):
        x[p] = x[p] * recip[p]
        for r in range(p):
            x[r] = x[r] - lu[r][p] * x[p]
    return x


def normalise(d_ref, x_ref, s):
    lu, recip = factor_rows([d_ref[s, r] for r in range(5)])
    x = solve_rows(lu, recip, [x_ref[s, r] for r in range(5)])
    for r in range(5):
        pieces = [lu[r][:r], recip[r][None], lu[r][r + 1 :]]
        d_ref[s, r] = jnp.concatenate([p for p in pieces if p.shape[0]], axis=0)
        x_ref[s, r] = x[r]


def solve_with(d_ref, s, right):
    lu = [d_ref[s, r] for r in range(5)]
    return solve_rows(lu, [lu[r][r] for r in range(5)], right)


def row_times(row, others):
    total = row[0] * others[0]
    for m in range(1, 5):
        total = total + row[m] * others[m]
    return total


def combine(own, diagonal, before, after, d_ref, x_ref, s):
    for r in range(5):
        left = row_times(own[r][:5], before)
        right = row_times(own[r][5:], after)
        d_ref[s, r] = diagonal[r] - left[5:] - right[:5]
        x_ref[s, r] = jnp.concatenate([-left[:5], -right[5:]], axis=0)


def subtract(own, r, before, after):
    return r - row_times(own[:5], before) - row_times(own[5:], after)


def kernel(
    state_ref, visc_ref, resid_ref, out_ref,
    st, vis, res, ss, gg, send_m, recv_m, send_r, recv_r, send_x, recv_x,
    prm, d1, x1, d2, x2, dp, xp, rr, xx,
    in_sem, halo_send, halo_recv, a2a_send, a2a_recv, own_sem,
):
    me = lax.axis_index("stream")
    z = lax.axis_index("normal")
    z_count = lax.axis_size("normal")
    z_up = lax.rem(z + 1, z_count)
    z_down = lax.rem(z + z_count - 1, z_count)

    loads = [
        pltpu.make_async_copy(state_ref, st.at[:, :, pl.ds(8, 16), :], in_sem.at[0]),
        pltpu.make_async_copy(visc_ref, vis, in_sem.at[1]),
        pltpu.make_async_copy(resid_ref, res, in_sem.at[2]),
    ]
    for load in loads:
        load.start()

    barrier = pltpu.get_barrier_semaphore()

    def greet(k, carry):
        pl.semaphore_signal(barrier, inc=1, device_id={"stream": lax.rem(me + k, N)}, device_id_type=MESH)
        return carry

    lax.fori_loop(1, N, greet, 0)
    for other in (z_up, z_down):
        pl.semaphore_signal(barrier, inc=1, device_id={"normal": other}, device_id_type=MESH)

    def message(buf, t):
        return buf.at[pl.ds(pl.multiple_of(t * R, R), R)]

    def exchange(send, recv, which):
        def go(k, carry):
            t = lax.rem(me + k, N)
            pltpu.make_async_remote_copy(
                src_ref=message(send, t), dst_ref=message(recv, me),
                send_sem=a2a_send.at[which], recv_sem=a2a_recv.at[which],
                device_id={"stream": t}, device_id_type=MESH,
            ).start()
            return carry

        lax.fori_loop(1, N, go, 0)
        pltpu.make_async_copy(message(send, me), message(recv, me), own_sem.at[which]).start()

    def all_of(send, recv, which):
        return pltpu.make_async_remote_copy(
            src_ref=send.at[pl.ds(0, (N - 1) * R)], dst_ref=recv.at[pl.ds(0, (N - 1) * R)],
            send_sem=a2a_send.at[which], recv_sem=a2a_recv.at[which],
            device_id={"stream": lax.rem(me + 1, N)}, device_id_type=MESH,
        )

    def arrived(send, recv, which):
        all_of(send, recv, which).wait_recv()
        pltpu.make_async_copy(message(send, me), message(recv, me), own_sem.at[which]).wait()

    def put(send, row, a, b):
        for h, rows in enumerate(swap_halves(a, b)):
            send[pl.ds(h * R + row, 16, stride=2 * R), :] = rows

    loads[0].wait()
    loads[1].wait()
    for c in range(2):
        pair = []
        for cell in (c, c + 2):
            rho, m1, m2, m3, energy = (st[p, cell, pl.ds(8, 16), :] for p in range(5))
            inverse = 1.0 / rho
            u, v, w = m1 * inverse, m2 * inverse, m3 * inverse
            h = 1.4 * energy * inverse - 0.2 * (u * u + v * v + w * w)
            pair.append((u, v, w, h, vis[cell]))
        for p in range(5):
            put(send_m, 2 * p + c, pair[0][p], pair[1][p])

    pl.semaphore_wait(barrier, N + 1)
    halos = [
        pltpu.make_async_remote_copy(
            src_ref=st.at[:, :, pl.ds(16, 8), :], dst_ref=st.at[:, :, pl.ds(0, 8), :],
            send_sem=halo_send.at[0], recv_sem=halo_recv.at[0],
            device_id={"normal": z_up}, device_id_type=MESH,
        ),
        pltpu.make_async_remote_copy(
            src_ref=st.at[:, :, pl.ds(8, 8), :], dst_ref=st.at[:, :, pl.ds(24, 8), :],
            send_sem=halo_send.at[1], recv_sem=halo_recv.at[1],
            device_id={"normal": z_down}, device_id_type=MESH,
        ),
    ]
    for halo in halos:
        halo.start()
    exchange(send_m, recv_m, 0)

    loads[2].wait()
    for halo in halos:
        halo.wait_recv()
    row = lax.broadcasted_iota(jnp.int32, (32, 128), 0)
    valid = (row >= jnp.where(z == 0, 8, 0)) & (row < jnp.where(z == z_count - 1, 24, 32))

    def right_side(c, carry):
        pair = []
        for cell in (c, c + 2):
            q = [st[p, cell] for p in range(5)]
            rho, m1, m2, m3, energy = q
            inverse = 1.0 / rho
            pressure = 0.4 * (energy - 0.5 * (m1 * m1 + m2 * m2 + m3 * m3) * inverse)
            v = m2 * inverse
            flux = [m2, m1 * v, m2 * v + pressure, m3 * v, (energy + pressure) * v]
            sigma = vis[cell]
            values = []
            for p in range(5):
                ss[p] = jnp.where(valid, q[p], 0.0)
                gg[p] = jnp.where(valid, flux[p], 0.0)
                s = {d: ss[p, pl.ds(8 + d, 16), :] for d in (-2, -1, 0, 1, 2)}
                values.append(
                    res[p, cell]
                    - 40.0 * (gg[p, pl.ds(9, 16), :] - gg[p, pl.ds(7, 16), :])
                    + sigma * (s[1] - 2.0 * s[0] + s[-1])
                    - 8.0 * (s[2] - 4.0 * s[1] + 6.0 * s[0] - 4.0 * s[-1] + s[-2])
                )
            pair.append(values)
        for p in range(5):
            put(send_r, 2 * p + c, pair[0][p], pair[1][p])
        return carry

    for c in range(2):
        right_side(c, 0)
    exchange(send_r, recv_r, 1)

    def get(recv, row, e):
        return swap_halves(*(recv[pl.ds((2 * b + e) * R + row, 8, stride=4 * R), :] for b in range(2)))

    arrived(send_m, recv_m, 0)
    for e in range(2):
        for c in range(2):
            both = [get(recv_m, 2 * p + c, e) for p in range(5)]
            for side in range(2):
                u, v, w, h, sigma = (both[p][side] for p in range(5))
                k = 0.5 * (u * u + v * v + w * w)
                cell = 4 * e + c + 2 * side
                values = (u, v, w, h, k, sigma, 1.0 / (1.0 + 2.0 * sigma))
                for p in range(7):
                    prm[p, cell + 2] = values[p]
                    if cell >= 6:
                        prm[p, cell - 6] = previous(values[p], 1)
                    if cell == 0:
                        prm[p, 10] = following(values[p], 1)

    def gas(place_):
        return tuple(prm[p, place_] for p in range(5))

    def level_1(i, carry):
        at = 2 * i + 2
        sigma, before, after = prm[5, at], prm[5, at - 1], prm[5, at + 1]
        left = scaled(jacobian_rows(*gas(at - 1)), sigma, prm[6, at - 1])
        right = scaled(jacobian_rows(*gas(at + 1)), -sigma, prm[6, at + 1])
        here, far_left, far_right = gas(at), gas(at - 2), gas(at + 2)
        for r in range(5):
            both = [plus(left[r][c], right[r][c]) for c in range(5)]
            own = row_times_jacobian(both, here, 0.0)
            for c in range(5):
                if left[r][c] is not None:
                    own[c] = own[c] + (after * right[r][c] - before * left[r][c])
            own[r] = own[r] + (1.0 + 2.0 * sigma)
            lower = row_times_jacobian(left[r], far_left, before)
            upper = row_times_jacobian(right[r], far_right, -after)
            for c in range(5):
                d1[i + 1, r, c] = own[c]
                x1[i + 1, r, c] = -lower[c]
                x1[i + 1, r, 5 + c] = -upper[c]
        return carry

    lax.fori_loop(0, 4, level_1, 0)

    def level_2_normalise(i, carry):
        normalise(d1, x1, 2 * i + 2)
        return carry

    lax.fori_loop(0, 2, level_2_normalise, 0)
    for r in range(5):
        x1[0, r] = previous(x1[4, r], 1)

    def rows_of(ref, s):
        return [ref[s, r] for r in range(5)]

    def level_2_combine(i, carry):
        s = 2 * i + 1
        combine(rows_of(x1, s), rows_of(d1, s), rows_of(x1, s - 1), rows_of(x1, s + 1), d2, x2, i)
        return carry

    lax.fori_loop(0, 2, level_2_combine, 0)

    normalise(d2, x2, 1)
    combine(
        rows_of(x2, 0), rows_of(d2, 0), [previous(x2[1, r], 1) for r in range(5)], rows_of(x2, 1), dp, xp, 0
    )

    unit = jnp.ones((8, 128), jnp.float32)
    nought = jnp.zeros((8, 128), jnp.float32)
    identity = [jnp.stack([unit if r == c else nought for c in range(5)]) for r in range(5)]
    for step in range(3):
        normalise(dp, xp, step)
        own = rows_of(xp, step)
        combine(
            own, identity, [previous(x, 2**step) for x in own], [following(x, 2**step) for x in own],
            dp, xp, step + 1,
        )
    lu, recip = factor_rows(rows_of(dp, 3))
    q, _ = place((5, 8, 128))
    other = [jnp.where(q < 4, xp[3, r, pl.ds(5, 5)], xp[3, r, pl.ds(0, 5)]) for r in range(5)]
    other = solve_rows(lu, recip, other)
    partner = [roll_rows(x, 4) for x in other]
    last, last_recip = factor_rows([identity[r] - row_times(other[r], partner) for r in range(5)])

    arrived(send_r, recv_r, 1)
    for e in range(2):
        for c in range(2):
            for p in range(5):
                a, b = get(recv_r, 2 * p + c, e)
                rr[4 * e + c, p] = a
                rr[4 * e + c + 2, p] = b

    def column(ref, i):
        return [ref[i, p] for p in range(5)]

    odd = {}
    for i in (1, 3, 5, 7):
        y = [prm[6, i + 2] * value for value in column(rr, i)]
        odd[i] = y, jacobian_times(gas(i + 2), y)
    odd[-1] = tuple([previous(value, 1) for value in part] for part in odd[7])
    even = {}
    for i in (0, 2, 4, 6):
        sigma = prm[5, i + 2]
        (y0, f0), (y1, f1) = odd[i - 1], odd[i + 1]
        even[i] = [rr[i, p] + sigma * (y0[p] + y1[p]) + (f0[p] - f1[p]) for p in range(5)]
    y = {i: solve_with(d1, i // 2 + 1, even[i]) for i in (2, 6)}
    y[-2] = [previous(value, 1) for value in y[6]]
    four = {}
    for i in (0, 4):
        four[i] = [subtract(x1[i // 2 + 1, r], even[i][r], y[i - 2], y[i + 2]) for r in range(5)]
    y[4] = solve_with(d2, 1, four[4])
    before = [previous(value, 1) for value in y[4]]
    b = [subtract(x2[0, r], four[0][r], before, y[4]) for r in range(5)]
    for step in range(3):
        b = solve_with(dp, step, b)
        before = [previous(value, 2**step) for value in b]
        after = [following(value, 2**step) for value in b]
        b = [subtract(xp[step, r], b[r], before, after) for r in range(5)]
    b = solve_rows(lu, recip, b)
    paired = [roll_rows(value, 4) for value in b]
    b = [b[r] - row_times(other[r], paired) for r in range(5)]
    x = {0: solve_rows(last, last_recip, b)}
    x[8] = [following(value, 1) for value in x[0]]
    x[4] = [subtract(x2[1, r], y[4][r], x[0], x[8]) for r in range(5)]
    for i in (2, 6):
        x[i] = [subtract(x1[i // 2 + 1, r], y[i][r], x[i - 2], x[i + 2]) for r in range(5)]
    flux = {i: jacobian_times(gas(i + 2), x[i]) for i in (0, 2, 4, 6)}
    flux[8] = [following(value, 1) for value in flux[0]]
    for i in (1, 3, 5, 7):
        sigma, inverse = prm[5, i + 2], prm[6, i + 2]
        x[i] = [
            inverse * (rr[i, p] + sigma * (x[i - 1][p] + x[i + 1][p]) + (flux[i - 1][p] - flux[i + 1][p]))
            for p in range(5)
        ]

    for e in range(2):
        for c in range(2):
            for p in range(5):
                parts = swap_halves(x[4 * e + c][p], x[4 * e + c + 2][p])
                for b in range(2):
                    send_x[pl.ds((2 * b + e) * R + 2 * p + c, 8, stride=4 * R), :] = parts[b]
    exchange(send_x, recv_x, 2)
    arrived(send_x, recv_x, 2)
    for c in range(2):
        for p in range(5):
            parts = [recv_x[pl.ds(h * R + 2 * p + c, 16, stride=2 * R), :] for h in range(2)]
            out_ref[p, c], out_ref[p, c + 2] = swap_halves(*parts)

    for halo in halos:
        halo.wait_send()
    for which, (send, recv) in enumerate(((send_m, recv_m), (send_r, recv_r), (send_x, recv_x))):
        all_of(send, recv, which).wait_send()


def on_device(state, viscosity, residual_other):
    f32 = jnp.float32
    tile = (8, 128)
    buffer = pltpu.VMEM((N * R, 128), f32)
    return pl.pallas_call(
        kernel,
        out_shape=jax.ShapeDtypeStruct(state.shape, f32),
        in_specs=[pl.BlockSpec(memory_space=pl.ANY)] * 3,
        out_specs=pl.BlockSpec(memory_space=pltpu.VMEM),
        scratch_shapes=[
            pltpu.VMEM((5, 4, 32, 128), f32),
            pltpu.VMEM((4, 16, 128), f32),
            pltpu.VMEM((5, 4, 16, 128), f32),
            pltpu.VMEM((5, 32, 128), f32),
            pltpu.VMEM((5, 32, 128), f32),
        ]
        + [buffer] * 6
        + [
            pltpu.VMEM((7, 11) + tile, f32),
            pltpu.VMEM((5, 5, 5) + tile, f32),
            pltpu.VMEM((5, 5, 10) + tile, f32),
            pltpu.VMEM((2, 5, 5) + tile, f32),
            pltpu.VMEM((2, 5, 10) + tile, f32),
            pltpu.VMEM((4, 5, 5) + tile, f32),
            pltpu.VMEM((4, 5, 10) + tile, f32),
            pltpu.VMEM((8, 5) + tile, f32),
            pltpu.VMEM((8, 5) + tile, f32),
            pltpu.SemaphoreType.DMA((3,)),
            pltpu.SemaphoreType.DMA((2,)),
            pltpu.SemaphoreType.DMA((2,)),
            pltpu.SemaphoreType.DMA((3,)),
            pltpu.SemaphoreType.DMA((3,)),
            pltpu.SemaphoreType.DMA((3,)),
        ],
        compiler_params=pltpu.CompilerParams(
            collective_id=0, has_side_effects=True, vmem_limit_bytes=32 * 1024 * 1024
        ),
    )(state, viscosity, residual_other)


def solution(mesh):
    placed = (
        P(None, "stream", "normal", None),
        P("stream", "normal", None),
        P(None, "stream", "normal", None),
    )
    return jax.shard_map(
        on_device,
        mesh=mesh,
        in_specs=placed,
        out_specs=P(None, "stream", "normal", None),
        check_vma=False,
    )
```

```python
import jax
import jax.numpy as jnp
from jax import lax
from jax.experimental import pallas as pl
from jax.experimental.pallas import tpu as pltpu
from jax.sharding import PartitionSpec as P

N = 32
R = 16
ROWS = 10
HALF = 64
MESH = pl.DeviceIdType.MESH


def roll_lanes(x):
    return pltpu.roll(x, HALF, axis=x.ndim - 1)


def roll_rows(x, by):
    return pltpu.roll(x, by % 8, axis=x.ndim - 2)


def swap_halves(a, b):
    low = lax.broadcasted_iota(jnp.int32, a.shape, a.ndim - 1) < HALF
    return jnp.where(low, a, roll_lanes(b)), jnp.where(low, roll_lanes(a), b)


def place(shape):
    q = lax.broadcasted_iota(jnp.int32, shape, len(shape) - 2)
    b = lax.broadcasted_iota(jnp.int32, shape, len(shape) - 1) >= HALF
    return q, b


def previous(x, by):
    q, b = place(x.shape)
    if by == 1:
        moved = roll_lanes(jnp.where(b, roll_rows(x, 1), x))
        return jnp.where((q == 0) & ~b, 0.0, moved)
    return jnp.where(q < by // 2, 0.0, roll_rows(x, by // 2))


def following(x, by):
    q, b = place(x.shape)
    if by == 1:
        moved = roll_lanes(jnp.where(b, x, roll_rows(x, -1)))
        return jnp.where((q == 7) & b, 0.0, moved)
    return jnp.where(q >= 8 - by // 2, 0.0, roll_rows(x, -(by // 2)))


def jacobian_rows(u, v, w, h, k):
    return [
        [None, 1.0, None, None, None],
        [0.4 * k - u * u, 1.6 * u, -0.4 * v, -0.4 * w, 0.4],
        [-u * v, v, u, None, None],
        [-u * w, w, None, u, None],
        [u * (0.4 * k - h), h - 0.4 * u * u, -0.4 * u * v, -0.4 * u * w, 1.4 * u],
    ]


def jacobian_times(prm, m):
    u, v, w, h, k = prm
    t = m[1] - u * m[0]
    p = 0.4 * (k * m[0] - u * m[1] - v * m[2] - w * m[3] + m[4])
    return [
        m[1],
        p + u * (m[1] + t),
        v * t + u * m[2],
        w * t + u * m[3],
        u * (p + m[4]) + h * t,
    ]


def row_times_jacobian(g, prm, shift):
    u, v, w, h, k = prm
    e = g[0]
    for value, factor in ((g[1], u), (g[2], v), (g[3], w), (g[4], h)):
        if value is not None:
            e = value * factor if e is None else e + value * factor
    p = g[1] if g[4] is None else g[1] + u * g[4]
    p = 0.4 * p
    s = u + shift

    def part(index, other):
        return other if g[index] is None else s * g[index] + other

    return [
        part(0, k * p - u * e),
        part(1, e - u * p),
        part(2, -(v * p)),
        part(3, -(w * p)),
        part(4, p),
    ]


def scaled(rows, shift, factor):
    out = []
    for r in range(5):
        row = []
        for c in range(5):
            value = rows[r][c]
            if r == c:
                value = shift if value is None else value + shift
            row.append(None if value is None else value * factor)
        out.append(row)
    return out


def plus(a, b):
    if a is None:
        return b
    return a if b is None else a + b


def factor_rows(rows):
    rows = list(rows)
    recip = []
    for p in range(5):
        rec = 1.0 / rows[p][p]
        recip.append(rec)
        for r in range(p + 1, 5):
            weight = rows[r][p] * rec
            tail = rows[r][p + 1 :] - weight[None] * rows[p][p + 1 :] if p < 4 else None
            parts = [rows[r][:p], weight[None], tail] if p else [weight[None], tail]
            rows[r] = jnp.concatenate(parts, axis=0)
    return rows, recip


def solve_rows(lu, recip, right):
    x = list(right)
    for p in range(5):
        for r in range(p + 1, 5):
            x[r] = x[r] - lu[r][p] * x[p]
    for p in range(4, -1, -1):
        x[p] = x[p] * recip[p]
        for r in range(p):
            x[r] = x[r] - lu[r][p] * x[p]
    return x


def normalise(d_ref, x_ref, s):
    lu, recip = factor_rows([d_ref[s, r] for r in range(5)])
    x = solve_rows(lu, recip, [x_ref[s, r] for r in range(5)])
    for r in range(5):
        pieces = [lu[r][:r], recip[r][None], lu[r][r + 1 :]]
        d_ref[s, r] = jnp.concatenate([p for p in pieces if p.shape[0]], axis=0)
        x_ref[s, r] = x[r]


def solve_with(d_ref, s, right):
    lu = [d_ref[s, r] for r in range(5)]
    return solve_rows(lu, [lu[r][r] for r in range(5)], right)


def row_times(row, others):
    total = row[0] * others[0]
    for m in range(1, 5):
        total = total + row[m] * others[m]
    return total


def combine(own, diagonal, before, after, d_ref, x_ref, s):
    for r in range(5):
        left = row_times(own[r][:5], before)
        right = row_times(own[r][5:], after)
        d_ref[s, r] = diagonal[r] - left[5:] - right[:5]
        x_ref[s, r] = jnp.concatenate([-left[:5], -right[5:]], axis=0)


def subtract(own, r, before, after):
    return r - row_times(own[:5], before) - row_times(own[5:], after)


def kernel(
    state_ref, visc_ref, resid_ref, out_ref,
    st, vis, res, halo, gg, send_m, recv_m, send_r, recv_r, send_x, recv_x,
    prm, d1, x1, d2, x2, dp, xp, rr,
    in_sem, halo_send, halo_recv, a2a_send, a2a_recv, own_sem,
):
    me = lax.axis_index("stream")
    z = lax.axis_index("normal")
    z_count = lax.axis_size("normal")

    def load(k, source, target):
        return pltpu.make_async_copy(source, target, in_sem.at[k])

    loads = [
        load(0, state_ref, st.at[:, :, pl.ds(8, 16), :]),
        load(1, visc_ref, vis),
        load(2, resid_ref, res),
    ]
    for each in loads:
        each.start()

    halo[...] = jnp.zeros_like(halo)
    for ends in (pl.ds(0, 8), pl.ds(24, 8)):
        st[:, :, ends, :] = jnp.zeros((5, 4, 8, 128), jnp.float32)
        gg[:, ends, :] = jnp.zeros((5, 8, 128), jnp.float32)

    has_up, has_down = z < z_count - 1, z > 0
    px, py, core = me // 8, (me // 2) % 4, me % 2

    def partner(i):
        return (px + 6 - i // 8) % 4 * 8 + (py + 6 - (i // 2) % 4) % 4 * 2 + (core + i) % 2

    def for_partners(action):
        def go(i, carry):
            action(partner(i))
            return carry

        lax.fori_loop(0, 20, go, 0)
        lax.fori_loop(21, N, go, 0)

    barrier = pltpu.get_barrier_semaphore()
    for_partners(lambda t: pl.semaphore_signal(barrier, inc=1, device_id={"stream": t}, device_id_type=MESH))

    @pl.when(has_up)
    def _():
        pl.semaphore_signal(barrier, inc=1, device_id={"normal": z + 1}, device_id_type=MESH)

    @pl.when(has_down)
    def _():
        pl.semaphore_signal(barrier, inc=1, device_id={"normal": z - 1}, device_id_type=MESH)

    def message(buf, t):
        return buf.at[pl.ds(pl.multiple_of(t * R, R), ROWS)]

    def send_to(send, recv, which, t):
        pltpu.make_async_remote_copy(
            src_ref=message(send, t), dst_ref=message(recv, me),
            send_sem=a2a_send.at[which], recv_sem=a2a_recv.at[which],
            device_id={"stream": t}, device_id_type=MESH,
        ).start()

    def own_copy(send, recv, which):
        return pltpu.make_async_copy(message(send, me), message(recv, me), own_sem.at[which])

    def exchange(send, recv, which):
        for_partners(lambda t: send_to(send, recv, which, t))
        own_copy(send, recv, which).start()

    def all_of(send, recv, which):
        return pltpu.make_async_remote_copy(
            src_ref=send.at[pl.ds(0, (N - 1) * ROWS)], dst_ref=recv.at[pl.ds(0, (N - 1) * ROWS)],
            send_sem=a2a_send.at[which], recv_sem=a2a_recv.at[which],
            device_id={"stream": lax.rem(me + 1, N)}, device_id_type=MESH,
        )

    def arrived(send, recv, which):
        all_of(send, recv, which).wait_recv()
        own_copy(send, recv, which).wait()

    def put(send, row, a, b):
        for h, rows in enumerate(swap_halves(a, b)):
            send[pl.ds(h * R + row, 16, stride=2 * R), :] = rows

    loads[0].wait()
    loads[1].wait()
    for c in range(2):
        pair = []
        for cell in (c, c + 2):
            rho, m1, m2, m3, energy = (st[p, cell, pl.ds(8, 16), :] for p in range(5))
            inverse = 1.0 / rho
            u, v, w = m1 * inverse, m2 * inverse, m3 * inverse
            h = 1.4 * energy * inverse - 0.2 * (u * u + v * v + w * w)
            pair.append((u, v, w, h, vis[cell]))
        for p in range(5):
            put(send_m, 2 * p + c, pair[0][p], pair[1][p])

    pl.semaphore_wait(barrier, N - 1 + has_up.astype(jnp.int32) + has_down.astype(jnp.int32))
    upward = pltpu.make_async_remote_copy(
        src_ref=state_ref.at[:, :, pl.ds(14, 2), :], dst_ref=halo.at[0, :, :, pl.ds(0, 2), :],
        send_sem=halo_send.at[0], recv_sem=halo_recv.at[0],
        device_id={"normal": lax.rem(z + 1, z_count)}, device_id_type=MESH,
    )
    downward = pltpu.make_async_remote_copy(
        src_ref=state_ref.at[:, :, pl.ds(0, 2), :], dst_ref=halo.at[1, :, :, pl.ds(6, 2), :],
        send_sem=halo_send.at[1], recv_sem=halo_recv.at[1],
        device_id={"normal": lax.rem(z + z_count - 1, z_count)}, device_id_type=MESH,
    )
    pl.when(has_up)(upward.start)
    pl.when(has_down)(downward.start)
    exchange(send_m, recv_m, 0)

    def flux_of(q):
        rho, m1, m2, m3, energy = q
        inverse = 1.0 / rho
        pressure = 0.4 * (energy - 0.5 * (m1 * m1 + m2 * m2 + m3 * m3) * inverse)
        v = m2 * inverse
        return [m2, m1 * v, m2 * v + pressure, m3 * v, (energy + pressure) * v]

    def differences(q, g):
        second = q(1) - 2.0 * q(0) + q(-1)
        fourth = q(2) - 4.0 * q(1) + 6.0 * q(0) - 4.0 * q(-1) + q(-2)
        return second, -40.0 * (g(1) - g(-1)) - 8.0 * fourth

    loads[2].wait()
    for c in range(2):
        pair = []
        for cell in (c, c + 2):
            q = [st[p, cell, pl.ds(8, 16), :] for p in range(5)]
            flux = flux_of(q)
            values = []
            for p in range(5):
                gg[p, pl.ds(8, 16)] = flux[p]
                second, rest = differences(
                    lambda d: st[p, cell, pl.ds(8 + d, 16), :], lambda d: gg[p, pl.ds(8 + d, 16), :]
                )
                values.append(res[p, cell] + vis[cell] * second + rest)
            pair.append(values)
        for p in range(5):
            put(send_r, 2 * p + c, pair[0][p], pair[1][p])

    def inner(t):
        @pl.when((t >= 4) & (t < N - 4))
        def _():
            send_to(send_r, recv_r, 1, t)

    for_partners(inner)

    pl.when(has_down)(upward.wait_recv)
    pl.when(has_up)(downward.wait_recv)
    index = lax.broadcasted_iota(jnp.int32, (8, 128), 0)
    for end in range(2):
        first, offset = 8 * end, -2 + 4 * end
        real = index < jnp.where(has_up, 8, 6) if end else index >= jnp.where(has_down, 0, 2)
        for c in range(2):
            pair = []
            for cell in (c, c + 2):
                q = [st[p, cell, pl.ds(6 + 12 * end, 8), :] + halo[end, p, cell] for p in range(5)]
                flux = flux_of([jnp.where(real, q[0], 1.0)] + q[1:])
                sigma = vis[cell, pl.ds(first, 8), :]
                values = []
                for p in range(5):
                    g = jnp.where(real, flux[p], 0.0)
                    second, rest = differences(lambda d: roll_rows(q[p], -d), lambda d: roll_rows(g, -d))
                    values.append(
                        res[p, cell, pl.ds(first, 8), :]
                        + sigma * roll_rows(second, offset)
                        + roll_rows(rest, offset)
                    )
                pair.append(values)
            for p in range(5):
                for h, rows in enumerate(swap_halves(pair[0][p], pair[1][p])):
                    at = (28 * end + h) * R + 2 * p + c
                    send_r[pl.ds(at, 2, stride=2 * R), :] = rows[6 * end : 6 * end + 2]

    def outer(i, carry):
        t = jnp.where(i < 4, i, i + N - 8)

        @pl.when(t != me)
        def _():
            send_to(send_r, recv_r, 1, t)

        return carry

    lax.fori_loop(0, 8, outer, 0)
    own_copy(send_r, recv_r, 1).start()

    def get(recv, row, e):
        return swap_halves(*(recv[pl.ds((2 * b + e) * R + row, 8, stride=4 * R), :] for b in range(2)))

    arrived(send_m, recv_m, 0)
    for e in range(2):
        for c in range(2):
            both = [get(recv_m, 2 * p + c, e) for p in range(5)]
            for side in range(2):
                u, v, w, h, sigma = (both[p][side] for p in range(5))
                k = 0.5 * (u * u + v * v + w * w)
                cell = 4 * e + c + 2 * side
                values = (u, v, w, h, k, sigma, 1.0 / (1.0 + 2.0 * sigma))
                for p in range(7):
                    prm[p, cell + 2] = values[p]
                    if cell >= 6:
                        prm[p, cell - 6] = previous(values[p], 1)
                    if cell == 0:
                        prm[p, 10] = following(values[p], 1)

    def gas(place_):
        return tuple(prm[p, place_] for p in range(5))

    def level_1(i, carry):
        at = 2 * i + 2
        sigma, before, after = prm[5, at], prm[5, at - 1], prm[5, at + 1]
        left = scaled(jacobian_rows(*gas(at - 1)), sigma, prm[6, at - 1])
        right = scaled(jacobian_rows(*gas(at + 1)), -sigma, prm[6, at + 1])
        here, far_left, far_right = gas(at), gas(at - 2), gas(at + 2)
        for r in range(5):
            both = [plus(left[r][c], right[r][c]) for c in range(5)]
            own = row_times_jacobian(both, here, 0.0)
            for c in range(5):
                if left[r][c] is not None:
                    own[c] = own[c] + (after * right[r][c] - before * left[r][c])
            own[r] = own[r] + (1.0 + 2.0 * sigma)
            lower = row_times_jacobian(left[r], far_left, before)
            upper = row_times_jacobian(right[r], far_right, -after)
            for c in range(5):
                d1[i + 1, r, c] = own[c]
                x1[i + 1, r, c] = -lower[c]
                x1[i + 1, r, 5 + c] = -upper[c]
        return carry

    lax.fori_loop(0, 4, level_1, 0)

    def level_2_normalise(i, carry):
        normalise(d1, x1, 2 * i + 2)
        return carry

    lax.fori_loop(0, 2, level_2_normalise, 0)
    for r in range(5):
        x1[0, r] = previous(x1[4, r], 1)

    def rows_of(ref, s):
        return [ref[s, r] for r in range(5)]

    def level_2_combine(i, carry):
        s = 2 * i + 1
        combine(rows_of(x1, s), rows_of(d1, s), rows_of(x1, s - 1), rows_of(x1, s + 1), d2, x2, i)
        return carry

    lax.fori_loop(0, 2, level_2_combine, 0)

    normalise(d2, x2, 1)
    combine(
        rows_of(x2, 0), rows_of(d2, 0), [previous(x2[1, r], 1) for r in range(5)], rows_of(x2, 1), dp, xp, 0
    )

    unit = jnp.ones((8, 128), jnp.float32)
    nought = jnp.zeros((8, 128), jnp.float32)
    identity = [jnp.stack([unit if r == c else nought for c in range(5)]) for r in range(5)]
    for step in range(3):
        normalise(dp, xp, step)
        own = rows_of(xp, step)
        combine(
            own, identity, [previous(x, 2**step) for x in own], [following(x, 2**step) for x in own],
            dp, xp, step + 1,
        )
    lu, recip = factor_rows(rows_of(dp, 3))
    q, _ = place((5, 8, 128))
    other = [jnp.where(q < 4, xp[3, r, pl.ds(5, 5)], xp[3, r, pl.ds(0, 5)]) for r in range(5)]
    other = solve_rows(lu, recip, other)
    facing = [roll_rows(x, 4) for x in other]
    last, last_recip = factor_rows([identity[r] - row_times(other[r], facing) for r in range(5)])

    arrived(send_r, recv_r, 1)
    for e in range(2):
        for c in range(2):
            for p in range(5):
                a, b = get(recv_r, 2 * p + c, e)
                rr[4 * e + c, p] = a
                rr[4 * e + c + 2, p] = b

    def column(ref, i):
        return [ref[i, p] for p in range(5)]

    odd = {}
    for i in (1, 3, 5, 7):
        y = [prm[6, i + 2] * value for value in column(rr, i)]
        odd[i] = y, jacobian_times(gas(i + 2), y)
    odd[-1] = tuple([previous(value, 1) for value in part] for part in odd[7])
    even = {}
    for i in (0, 2, 4, 6):
        sigma = prm[5, i + 2]
        (y0, f0), (y1, f1) = odd[i - 1], odd[i + 1]
        even[i] = [rr[i, p] + sigma * (y0[p] + y1[p]) + (f0[p] - f1[p]) for p in range(5)]
    y = {i: solve_with(d1, i // 2 + 1, even[i]) for i in (2, 6)}
    y[-2] = [previous(value, 1) for value in y[6]]
    four = {}
    for i in (0, 4):
        four[i] = [subtract(x1[i // 2 + 1, r], even[i][r], y[i - 2], y[i + 2]) for r in range(5)]
    y[4] = solve_with(d2, 1, four[4])
    before = [previous(value, 1) for value in y[4]]
    b = [subtract(x2[0, r], four[0][r], before, y[4]) for r in range(5)]
    for step in range(3):
        b = solve_with(dp, step, b)
        before = [previous(value, 2**step) for value in b]
        after = [following(value, 2**step) for value in b]
        b = [subtract(xp[step, r], b[r], before, after) for r in range(5)]
    b = solve_rows(lu, recip, b)
    paired = [roll_rows(value, 4) for value in b]
    b = [b[r] - row_times(other[r], paired) for r in range(5)]
    x = {0: solve_rows(last, last_recip, b)}
    x[8] = [following(value, 1) for value in x[0]]
    x[4] = [subtract(x2[1, r], y[4][r], x[0], x[8]) for r in range(5)]
    for i in (2, 6):
        x[i] = [subtract(x1[i // 2 + 1, r], y[i][r], x[i - 2], x[i + 2]) for r in range(5)]
    flux = {i: jacobian_times(gas(i + 2), x[i]) for i in (0, 2, 4, 6)}
    flux[8] = [following(value, 1) for value in flux[0]]
    for i in (1, 3, 5, 7):
        sigma, inverse = prm[5, i + 2], prm[6, i + 2]
        x[i] = [
            inverse * (rr[i, p] + sigma * (x[i - 1][p] + x[i + 1][p]) + (flux[i - 1][p] - flux[i + 1][p]))
            for p in range(5)
        ]

    for e in range(2):
        for c in range(2):
            for p in range(5):
                parts = swap_halves(x[4 * e + c][p], x[4 * e + c + 2][p])
                for b in range(2):
                    send_x[pl.ds((2 * b + e) * R + 2 * p + c, 8, stride=4 * R), :] = parts[b]
    exchange(send_x, recv_x, 2)
    arrived(send_x, recv_x, 2)
    for c in range(2):
        for p in range(5):
            parts = [recv_x[pl.ds(h * R + 2 * p + c, 16, stride=2 * R), :] for h in range(2)]
            out_ref[p, c], out_ref[p, c + 2] = swap_halves(*parts)

    pl.when(has_up)(upward.wait_send)
    pl.when(has_down)(downward.wait_send)
    for which, (send, recv) in enumerate(((send_m, recv_m), (send_r, recv_r), (send_x, recv_x))):
        all_of(send, recv, which).wait_send()


def on_device(state, viscosity, residual_other):
    f32 = jnp.float32
    tile = (8, 128)
    buffer = pltpu.VMEM((N * R, 128), f32)
    return pl.pallas_call(
        kernel,
        out_shape=jax.ShapeDtypeStruct(state.shape, f32),
        in_specs=[pl.BlockSpec(memory_space=pltpu.HBM)] * 3,
        out_specs=pl.BlockSpec(memory_space=pltpu.VMEM),
        scratch_shapes=[
            pltpu.VMEM((5, 4, 32, 128), f32),
            pltpu.VMEM((4, 16, 128), f32),
            pltpu.VMEM((5, 4, 16, 128), f32),
            pltpu.VMEM((2, 5, 4, 8, 128), f32),
            pltpu.VMEM((5, 32, 128), f32),
        ]
        + [buffer, buffer, pltpu.VMEM((3 * N * R // 2, 128), f32), buffer, buffer, buffer]
        + [
            pltpu.VMEM((7, 11) + tile, f32),
            pltpu.VMEM((5, 5, 5) + tile, f32),
            pltpu.VMEM((5, 5, 10) + tile, f32),
            pltpu.VMEM((2, 5, 5) + tile, f32),
            pltpu.VMEM((2, 5, 10) + tile, f32),
            pltpu.VMEM((4, 5, 5) + tile, f32),
            pltpu.VMEM((4, 5, 10) + tile, f32),
            pltpu.VMEM((8, 5) + tile, f32),
            pltpu.SemaphoreType.DMA((3,)),
            pltpu.SemaphoreType.DMA((2,)),
            pltpu.SemaphoreType.DMA((2,)),
            pltpu.SemaphoreType.DMA((3,)),
            pltpu.SemaphoreType.DMA((3,)),
            pltpu.SemaphoreType.DMA((3,)),
        ],
        compiler_params=pltpu.CompilerParams(
            collective_id=0, has_side_effects=True, vmem_limit_bytes=32 * 1024 * 1024
        ),
    )(*(pltpu.with_memory_space_constraint(x, pltpu.HBM) for x in (state, viscosity, residual_other)))


def solution(mesh):
    placed = (
        P(None, "stream", "normal", None),
        P("stream", "normal", None),
        P(None, "stream", "normal", None),
    )
    return jax.shard_map(
        on_device,
        mesh=mesh,
        in_specs=placed,
        out_specs=P(None, "stream", "normal", None),
        check_vma=False,
    )
```

```python
import jax
import jax.numpy as jnp
from jax import lax
from jax.experimental import pallas as pl
from jax.experimental.pallas import tpu as pltpu
from jax.sharding import PartitionSpec as P

N = 32
R = 16
ROWS = (10, 5, 5)
HALF = 64
MESH = pl.DeviceIdType.MESH


def roll_lanes(x):
    return pltpu.roll(x, HALF, axis=x.ndim - 1)


def roll_rows(x, by):
    return pltpu.roll(x, by % 8, axis=x.ndim - 2)


def swap_halves(a, b):
    low = lax.broadcasted_iota(jnp.int32, a.shape, a.ndim - 1) < HALF
    return jnp.where(low, a, roll_lanes(b)), jnp.where(low, roll_lanes(a), b)


def place(shape):
    q = lax.broadcasted_iota(jnp.int32, shape, len(shape) - 2)
    b = lax.broadcasted_iota(jnp.int32, shape, len(shape) - 1) >= HALF
    return q, b


def previous(x, by):
    q, b = place(x.shape)
    if by == 1:
        moved = roll_lanes(jnp.where(b, roll_rows(x, 1), x))
        return jnp.where((q == 0) & ~b, 0.0, moved)
    return jnp.where(q < by // 2, 0.0, roll_rows(x, by // 2))


def following(x, by):
    q, b = place(x.shape)
    if by == 1:
        moved = roll_lanes(jnp.where(b, x, roll_rows(x, -1)))
        return jnp.where((q == 7) & b, 0.0, moved)
    return jnp.where(q >= 8 - by // 2, 0.0, roll_rows(x, -(by // 2)))


def jacobian_rows(u, v, w, h, k):
    return [
        [None, 1.0, None, None, None],
        [0.4 * k - u * u, 1.6 * u, -0.4 * v, -0.4 * w, 0.4],
        [-u * v, v, u, None, None],
        [-u * w, w, None, u, None],
        [u * (0.4 * k - h), h - 0.4 * u * u, -0.4 * u * v, -0.4 * u * w, 1.4 * u],
    ]


def jacobian_times(prm, m):
    u, v, w, h, k = prm
    t = m[1] - u * m[0]
    p = 0.4 * (k * m[0] - u * m[1] - v * m[2] - w * m[3] + m[4])
    return [
        m[1],
        p + u * (m[1] + t),
        v * t + u * m[2],
        w * t + u * m[3],
        u * (p + m[4]) + h * t,
    ]


def row_times_jacobian(g, prm, shift):
    u, v, w, h, k = prm
    e = g[0]
    for value, factor in ((g[1], u), (g[2], v), (g[3], w), (g[4], h)):
        if value is not None:
            e = value * factor if e is None else e + value * factor
    p = g[1] if g[4] is None else g[1] + u * g[4]
    p = 0.4 * p
    s = u + shift

    def part(index, other):
        return other if g[index] is None else s * g[index] + other

    return [
        part(0, k * p - u * e),
        part(1, e - u * p),
        part(2, -(v * p)),
        part(3, -(w * p)),
        part(4, p),
    ]


def scaled(rows, shift, factor):
    out = []
    for r in range(5):
        row = []
        for c in range(5):
            value = rows[r][c]
            if r == c:
                value = shift if value is None else value + shift
            row.append(None if value is None else value * factor)
        out.append(row)
    return out


def plus(a, b):
    if a is None:
        return b
    return a if b is None else a + b


def shifted(prm, m, shift):
    return [a + shift * b for a, b in zip(jacobian_times(prm, m), m)]


def diagonal_rows(left, right, here, before, sigma, after):
    rows = []
    for r in range(5):
        own = row_times_jacobian([plus(left[r][c], right[r][c]) for c in range(5)], here, 0.0)
        for c in range(5):
            if left[r][c] is not None:
                own[c] = own[c] + (after * right[r][c] - before * left[r][c])
        own[r] = own[r] + (1.0 + 2.0 * sigma)
        rows.append(own)
    return rows


def factor_rows(rows):
    rows = list(rows)
    recip = []
    for p in range(5):
        rec = 1.0 / rows[p][p]
        recip.append(rec)
        for r in range(p + 1, 5):
            weight = rows[r][p] * rec
            tail = rows[r][p + 1 :] - weight[None] * rows[p][p + 1 :] if p < 4 else None
            parts = [rows[r][:p], weight[None], tail] if p else [weight[None], tail]
            rows[r] = jnp.concatenate(parts, axis=0)
    return rows, recip


def solve_rows(lu, recip, right):
    x = list(right)
    for p in range(5):
        for r in range(p + 1, 5):
            x[r] = x[r] - lu[r][p] * x[p]
    for p in range(4, -1, -1):
        x[p] = x[p] * recip[p]
        for r in range(p):
            x[r] = x[r] - lu[r][p] * x[p]
    return x


def identity(like):
    one, zero = jnp.ones_like(like), jnp.zeros_like(like)
    return [jnp.stack([one if r == c else zero for c in range(5)]) for r in range(5)]


def inverse_of(rows):
    return solve_rows(*factor_rows(rows), identity(rows[0][0]))


def normalise(d_ref, x_ref, s):
    rows = [d_ref[s, r] for r in range(5)]
    unit = identity(rows[0][0])
    x = solve_rows(*factor_rows(rows), [jnp.concatenate([x_ref[s, r], unit[r]], axis=0) for r in range(5)])
    for r in range(5):
        x_ref[s, r], d_ref[s, r] = x[r][:10], x[r][10:]


def times(rows, m):
    return [row_times(row, m) for row in rows]


def row_times(row, others):
    first = row[0] * others[0] + row[1] * others[1]
    return first + (row[2] * others[2] + row[3] * others[3]) + row[4] * others[4]


def combine(own, diagonal, before, after, d_ref, x_ref, s):
    for r in range(5):
        left = row_times(own[r][:5], before)
        right = row_times(own[r][5:], after)
        d_ref[s, r] = diagonal[r] - left[5:] - right[:5]
        x_ref[s, r] = jnp.concatenate([-left[:5], -right[5:]], axis=0)


def subtract(own, r, before, after):
    return r - (row_times(own[:5], before) + row_times(own[5:], after))


def kernel(
    state_ref, visc_ref, resid_ref, out_ref,
    st, vis, res, ro, halo, gg, send_m, recv_m, send_r, recv_r, send_x, recv_x,
    prm, d1, l1, d2, l2, dp, lp,
    in_sem, halo_send, halo_recv, a2a_send, a2a_recv, own_sem,
):
    me = lax.axis_index("stream")
    z = lax.axis_index("normal")
    z_count = lax.axis_size("normal")

    def load(k, source, target):
        return pltpu.make_async_copy(source, target, in_sem.at[k])

    loads = [
        load(0, state_ref, st.at[:, :, pl.ds(8, 16), :]),
        load(1, visc_ref, vis),
        load(2, resid_ref, res),
    ]
    for each in loads:
        each.start()

    halo[...] = jnp.zeros_like(halo)
    has_up, has_down = z < z_count - 1, z > 0
    px, py, core = me // 8, (me // 2) % 4, me % 2

    def partner(i):
        return (px + 6 - i // 8) % 4 * 8 + (py + 6 - (i // 2) % 4) % 4 * 2 + (core + i) % 2

    def for_partners(action):
        def go(i, carry):
            action(partner(i))
            return carry

        lax.fori_loop(0, 20, go, 0)
        lax.fori_loop(21, N, go, 0)

    barrier = pltpu.get_barrier_semaphore()

    @pl.when(has_up)
    def _():
        pl.semaphore_signal(barrier, inc=1, device_id={"normal": z + 1}, device_id_type=MESH)

    @pl.when(has_down)
    def _():
        pl.semaphore_signal(barrier, inc=1, device_id={"normal": z - 1}, device_id_type=MESH)

    for_partners(lambda t: pl.semaphore_signal(barrier, inc=1, device_id={"stream": t}, device_id_type=MESH))
    for ends in (pl.ds(0, 8), pl.ds(24, 8)):
        st[:, :, ends, :] = jnp.zeros((5, 4, 8, 128), jnp.float32)
        gg[:, ends, :] = jnp.zeros((5, 8, 128), jnp.float32)

    slot = lax.rem(me + N - 4, N)

    def message(buf, which, t):
        return buf.at[pl.ds(pl.multiple_of(t * R, R), ROWS[which])]

    def slot_of(t):
        return lax.rem(t + N - 4, N)

    def there(send, recv, which, t):
        if which == 2:
            return message(send, which, t), message(recv, which, slot)
        return message(send, which, slot_of(t)), message(recv, which, me)

    def own_copy(send, recv, which):
        return pltpu.make_async_copy(*there(send, recv, which, me), own_sem.at[which])

    def send_to(send, recv, which, t):
        source, target = there(send, recv, which, t)
        pltpu.make_async_remote_copy(
            src_ref=source, dst_ref=target,
            send_sem=a2a_send.at[which], recv_sem=a2a_recv.at[which],
            device_id={"stream": t}, device_id_type=MESH,
        ).start()

    def exchange(send, recv, which):
        for_partners(lambda t: send_to(send, recv, which, t))
        own_copy(send, recv, which).start()

    def all_of(send, recv, which):
        return pltpu.make_async_remote_copy(
            src_ref=send.at[pl.ds(0, (N - 1) * ROWS[which])], dst_ref=recv.at[pl.ds(0, (N - 1) * ROWS[which])],
            send_sem=a2a_send.at[which], recv_sem=a2a_recv.at[which],
            device_id={"stream": lax.rem(me + 1, N)}, device_id_type=MESH,
        )

    def arrived(send, recv, which):
        all_of(send, recv, which).wait_recv()
        own_copy(send, recv, which).wait()

    def put(send, row, a, b):
        for h, rows in enumerate(swap_halves(a, b)):
            send[pl.ds(h * R + row, 16, stride=2 * R), :] = rows

    loads[0].wait()
    loads[1].wait()
    gas_own, sig = [], [vis[cell] for cell in range(4)]
    for cell in range(4):
        rho, m1, m2, m3, energy = (st[p, cell, pl.ds(8, 16), :] for p in range(5))
        inverse = 1.0 / rho
        u, v, w = m1 * inverse, m2 * inverse, m3 * inverse
        k = 0.5 * (u * u + v * v + w * w)
        gas_own.append((u, v, w, 1.4 * energy * inverse - 0.4 * k, k))
    for c in range(2):
        for p in range(4):
            put(send_m, 2 * p + c, gas_own[c][p], gas_own[c + 2][p])
        put(send_m, 8 + c, sig[c], sig[c + 2])

    def flux_of(q):
        rho, m1, m2, m3, energy = q
        inverse = 1.0 / rho
        pressure = 0.4 * (energy - 0.5 * (m1 * m1 + m2 * m2 + m3 * m3) * inverse)
        v = m2 * inverse
        return [m2, m1 * v, m2 * v + pressure, m3 * v, (energy + pressure) * v]

    loads[2].wait()
    for cell in range(4):
        flux = flux_of([st[p, cell, pl.ds(8, 16), :] for p in range(5)])
        for p in range(5):
            gg[p, pl.ds(8, 16)] = flux[p]
            s = {d: st[p, cell, pl.ds(8 + d, 16), :] for d in (-2, -1, 0, 1, 2)}
            g = {d: gg[p, pl.ds(8 + d, 16), :] for d in (-1, 1)}
            ro[cell, p] = (
                res[p, cell]
                - 40.0 * (g[1] - g[-1])
                + vis[cell] * (s[1] - 2.0 * s[0] + s[-1])
                - 8.0 * (s[2] - 4.0 * s[1] + 6.0 * s[0] - 4.0 * s[-1] + s[-2])
            )

    inv1, inv3 = (1.0 / (1.0 + 2.0 * sig[cell]) for cell in (1, 3))
    own_inverse = inverse_of([
        jnp.stack(values)
        for values in diagonal_rows(
            scaled(jacobian_rows(*gas_own[1]), sig[2], inv1), scaled(jacobian_rows(*gas_own[3]), -sig[2], inv3),
            gas_own[2], sig[1], sig[2], sig[3],
        )
    ])

    def around(y1, x2, y3):
        flux = jacobian_times(gas_own[2], x2)
        x1 = [y1[p] - inv1 * (flux[p] - sig[1] * x2[p]) for p in range(5)]
        return x1, [y3[p] + inv3 * (flux[p] + sig[3] * x2[p]) for p in range(5)]

    def to_cell_2(y1, y3):
        a, b = shifted(gas_own[1], y1, sig[2]), shifted(gas_own[3], y3, -sig[2])
        return [a[p] - b[p] for p in range(5)]

    def condensed():
        y1, y3 = [inv1 * ro[1, p] for p in range(5)], [inv3 * ro[3, p] for p in range(5)]
        t = to_cell_2(y1, y3)
        x2 = times(own_inverse, [ro[2, p] + t[p] for p in range(5)])
        x1, x3 = around(y1, x2, y3)
        t = shifted(gas_own[1], x1, -sig[0])
        return [ro[0, p] - t[p] for p in range(5)], x3, y1, x2, y3

    rest, x3, *_ = condensed()
    for p in range(5):
        put(send_r, p, rest[p], x3[p])

    pl.semaphore_wait(barrier, N - 1 + has_up.astype(jnp.int32) + has_down.astype(jnp.int32))
    upward = pltpu.make_async_remote_copy(
        src_ref=state_ref.at[:, :, pl.ds(14, 2), :], dst_ref=halo.at[:, :, pl.ds(0, 2), :],
        send_sem=halo_send.at[0], recv_sem=halo_recv.at[0],
        device_id={"normal": lax.rem(z + 1, z_count)}, device_id_type=MESH,
    )
    downward = pltpu.make_async_remote_copy(
        src_ref=state_ref.at[:, :, pl.ds(0, 2), :], dst_ref=halo.at[:, :, pl.ds(6, 2), :],
        send_sem=halo_send.at[1], recv_sem=halo_recv.at[1],
        device_id={"normal": lax.rem(z + z_count - 1, z_count)}, device_id_type=MESH,
    )
    pl.when(has_up)(upward.start)
    pl.when(has_down)(downward.start)
    exchange(send_m, recv_m, 0)

    def inner(t):
        @pl.when(t >= 8)
        def _():
            send_to(send_r, recv_r, 1, t)

    for_partners(inner)

    pl.when(has_down)(upward.wait_recv)
    pl.when(has_up)(downward.wait_recv)
    index = lax.broadcasted_iota(jnp.int32, (8, 128), 0)
    low = index < 4
    edge = (index == 0) | (index == 7)

    def inward(plane):
        return jnp.where(low, roll_rows(plane, -1), roll_rows(plane, 1))

    for cell in range(4):
        q = [halo[p, cell] for p in range(5)]
        flux = flux_of([jnp.where(q[0] > 0.0, q[0], 1.0)] + q[1:])
        factor = 32.0 + jnp.where(low, vis[cell, pl.ds(0, 8), :], vis[cell, pl.ds(8, 8), :])
        for p in range(5):
            change = jnp.where(edge, factor * inward(q[p]) + jnp.where(low, 40.0, -40.0) * inward(flux[p]), 0.0)
            change = change - 8.0 * q[p]
            ro[cell, p, pl.ds(0, 8), :] = ro[cell, p, pl.ds(0, 8), :] + jnp.where(low, change, 0.0)
            ro[cell, p, pl.ds(8, 8), :] = ro[cell, p, pl.ds(8, 8), :] + jnp.where(low, 0.0, change)
    rest, x3, y1, x2, y3 = condensed()
    for p in range(5):
        for h, rows in enumerate(swap_halves(rest[p], x3[p])):
            for end in range(2):
                send_r[pl.ds((28 * end + h) * R + p, 2, stride=2 * R), :] = rows[14 * end : 14 * end + 2]

    def outer(t, carry):
        @pl.when(t != me)
        def _():
            send_to(send_r, recv_r, 1, t)

        return carry

    lax.fori_loop(0, 8, outer, 0)
    own_copy(send_r, recv_r, 1).start()

    def get(recv, row, e):
        return swap_halves(*(recv[pl.ds((2 * b + e) * R + row, 8, stride=4 * R), :] for b in range(2)))

    arrived(send_m, recv_m, 0)
    for e in range(2):
        for c in range(2):
            both = [get(recv_m, 2 * p + c, e) for p in range(5)]
            for side in range(2):
                u, v, w, h, sigma = (both[p][side] for p in range(5))
                k = 0.5 * (u * u + v * v + w * w)
                cell = 4 * e + c + 2 * side
                values = (u, v, w, h, k, sigma, 1.0 / (1.0 + 2.0 * sigma))
                for p in range(7):
                    prm[p, cell + 2] = values[p]
                    if cell >= 6:
                        prm[p, cell - 6] = previous(values[p], 1)
                    if cell == 0:
                        prm[p, 10] = following(values[p], 1)

    def gas(place_):
        return tuple(prm[p, place_] for p in range(5))

    def level_1(i, carry):
        at = 2 * i + 2
        sigma, before, after = prm[5, at], prm[5, at - 1], prm[5, at + 1]
        left = scaled(jacobian_rows(*gas(at - 1)), sigma, prm[6, at - 1])
        right = scaled(jacobian_rows(*gas(at + 1)), -sigma, prm[6, at + 1])
        here, far_left, far_right = gas(at), gas(at - 2), gas(at + 2)
        own = diagonal_rows(left, right, here, before, sigma, after)
        for r in range(5):
            lower = row_times_jacobian(left[r], far_left, before)
            upper = row_times_jacobian(right[r], far_right, -after)
            for c in range(5):
                d1[i + 1, r, c] = own[r][c]
                l1[i + 1, r, c] = -lower[c]
                l1[i + 1, r, 5 + c] = -upper[c]
        return carry

    lax.fori_loop(0, 4, level_1, 0)

    def level_2_normalise(i, carry):
        normalise(d1, l1, 2 * i + 2)
        return carry

    lax.fori_loop(0, 2, level_2_normalise, 0)
    for r in range(5):
        l1[0, r] = previous(l1[4, r], 1)

    def rows_of(ref, s):
        return [ref[s, r] for r in range(5)]

    def level_2_combine(i, carry):
        s = 2 * i + 1
        combine(rows_of(l1, s), rows_of(d1, s), rows_of(l1, s - 1), rows_of(l1, s + 1), d2, l2, i)
        return carry

    lax.fori_loop(0, 2, level_2_combine, 0)

    normalise(d2, l2, 1)
    combine(
        rows_of(l2, 0), rows_of(d2, 0), [previous(l2[1, r], 1) for r in range(5)], rows_of(l2, 1), dp, lp, 0
    )

    unit = identity(jnp.ones((8, 128), jnp.float32))
    for step in range(3):
        normalise(dp, lp, step)
        own = rows_of(lp, step)
        combine(
            own, unit, [previous(x, 2**step) for x in own], [following(x, 2**step) for x in own],
            dp, lp, step + 1,
        )
    q, _ = place((5, 8, 128))
    other = [jnp.where(q < 4, lp[3, r, pl.ds(5, 5)], lp[3, r, pl.ds(0, 5)]) for r in range(5)]
    both = solve_rows(*factor_rows(rows_of(dp, 3)), [jnp.concatenate([other[r], unit[r]], axis=0) for r in range(5)])
    other, fourth = [row[:5] for row in both], [row[5:] for row in both]
    facing = [roll_rows(x, 4) for x in other]
    last = inverse_of([unit[r] - row_times(other[r], facing) for r in range(5)])

    arrived(send_r, recv_r, 1)
    parts = [[get(recv_r, p, e) for p in range(5)] for e in range(2)]
    inside = [[parts[e][p][1] for p in range(5)] for e in range(2)]
    four = {}
    for i, before in ((0, [previous(value, 1) for value in inside[1]]), (4, inside[0])):
        t = shifted(gas(i + 1), before, prm[5, i + 2])
        four[i] = [parts[i // 4][p][0] + t[p] for p in range(5)]
    y = {}
    y[4] = times(rows_of(d2, 1), four[4])
    before = [previous(value, 1) for value in y[4]]
    b = [subtract(l2[0, r], four[0][r], before, y[4]) for r in range(5)]
    for step in range(3):
        b = times(rows_of(dp, step), b)
        before = [previous(value, 2**step) for value in b]
        after = [following(value, 2**step) for value in b]
        b = [subtract(lp[step, r], b[r], before, after) for r in range(5)]
    b = times(fourth, b)
    paired = [roll_rows(value, 4) for value in b]
    b = [b[r] - row_times(other[r], paired) for r in range(5)]
    x = {0: times(last, b)}
    x[8] = [following(value, 1) for value in x[0]]
    x[4] = [subtract(l2[1, r], y[4][r], x[0], x[8]) for r in range(5)]

    for e in range(2):
        beyond = shifted(gas(4 * e + 6), x[4 * e + 4], -prm[5, 4 * e + 5])
        for p in range(5):
            for b, rows in enumerate(swap_halves(x[4 * e][p], beyond[p])):
                send_x[pl.ds((2 * b + e) * R + p, 8, stride=4 * R), :] = rows
    exchange(send_x, recv_x, 2)
    arrived(send_x, recv_x, 2)
    both = [swap_halves(*(recv_x[pl.ds(h * R + p, 16, stride=2 * R), :] for h in range(2))) for p in range(5)]
    x0 = [both[p][0] for p in range(5)]
    after = [inv3 * both[p][1] for p in range(5)]
    before = [inv1 * value for value in shifted(gas_own[0], x0, sig[1])]
    t = times(own_inverse, to_cell_2(before, [-value for value in after]))
    x2 = [x2[p] + t[p] for p in range(5)]
    x1, x3 = around([y1[p] + before[p] for p in range(5)], x2, [y3[p] - after[p] for p in range(5)])
    for p in range(5):
        out_ref[p, 0], out_ref[p, 1], out_ref[p, 2], out_ref[p, 3] = x0[p], x1[p], x2[p], x3[p]

    pl.when(has_up)(upward.wait_send)
    pl.when(has_down)(downward.wait_send)
    for which, (send, recv) in enumerate(((send_m, recv_m), (send_r, recv_r), (send_x, recv_x))):
        all_of(send, recv, which).wait_send()


def on_device(state, viscosity, residual_other):
    f32 = jnp.float32
    tile = (8, 128)
    buffer = pltpu.VMEM((N * R, 128), f32)
    return pl.pallas_call(
        kernel,
        out_shape=jax.ShapeDtypeStruct(state.shape, f32),
        in_specs=[pl.BlockSpec(memory_space=pltpu.HBM)] * 3,
        out_specs=pl.BlockSpec(memory_space=pltpu.VMEM),
        scratch_shapes=[
            pltpu.VMEM((5, 4, 32, 128), f32),
            pltpu.VMEM((4, 16, 128), f32),
            pltpu.VMEM((5, 4, 16, 128), f32),
            pltpu.VMEM((4, 5, 16, 128), f32),
            pltpu.VMEM((5, 4, 8, 128), f32),
            pltpu.VMEM((5, 32, 128), f32),
        ]
        + [buffer, buffer, pltpu.VMEM((3 * N * R // 2, 128), f32), buffer, buffer, buffer]
        + [
            pltpu.VMEM((7, 11) + tile, f32),
            pltpu.VMEM((5, 5, 5) + tile, f32),
            pltpu.VMEM((5, 5, 10) + tile, f32),
            pltpu.VMEM((2, 5, 5) + tile, f32),
            pltpu.VMEM((2, 5, 10) + tile, f32),
            pltpu.VMEM((4, 5, 5) + tile, f32),
            pltpu.VMEM((4, 5, 10) + tile, f32),
            pltpu.SemaphoreType.DMA((3,)),
            pltpu.SemaphoreType.DMA((2,)),
            pltpu.SemaphoreType.DMA((2,)),
            pltpu.SemaphoreType.DMA((3,)),
            pltpu.SemaphoreType.DMA((3,)),
            pltpu.SemaphoreType.DMA((3,)),
        ],
        compiler_params=pltpu.CompilerParams(
            collective_id=0, has_side_effects=True, vmem_limit_bytes=32 * 1024 * 1024
        ),
    )(*(pltpu.with_memory_space_constraint(x, pltpu.HBM) for x in (state, viscosity, residual_other)))


def solution(mesh):
    placed = (
        P(None, "stream", "normal", None),
        P("stream", "normal", None),
        P(None, "stream", "normal", None),
    )
    return jax.shard_map(
        on_device,
        mesh=mesh,
        in_specs=placed,
        out_specs=P(None, "stream", "normal", None),
        check_vma=False,
    )
```

```python
import jax
import jax.numpy as jnp
from jax import lax
from jax.experimental import pallas as pl
from jax.experimental.pallas import tpu as pltpu
from jax.sharding import PartitionSpec as P

N = 32
R = 16
ROWS = (10, 5, 5)
HALF = 64
MESH = pl.DeviceIdType.MESH


def roll_lanes(x):
    return pltpu.roll(x, HALF, axis=x.ndim - 1)


def roll_rows(x, by):
    return pltpu.roll(x, by % 8, axis=x.ndim - 2)


def swap_halves(a, b):
    low = lax.broadcasted_iota(jnp.int32, a.shape, a.ndim - 1) < HALF
    return jnp.where(low, a, roll_lanes(b)), jnp.where(low, roll_lanes(a), b)


def place(shape):
    q = lax.broadcasted_iota(jnp.int32, shape, len(shape) - 2)
    b = lax.broadcasted_iota(jnp.int32, shape, len(shape) - 1) >= HALF
    return q, b


def previous(x, by):
    q, b = place(x.shape)
    if by == 1:
        moved = roll_lanes(jnp.where(b, roll_rows(x, 1), x))
        return jnp.where((q == 0) & ~b, 0.0, moved)
    return jnp.where(q < by // 2, 0.0, roll_rows(x, by // 2))


def following(x, by):
    q, b = place(x.shape)
    if by == 1:
        moved = roll_lanes(jnp.where(b, x, roll_rows(x, -1)))
        return jnp.where((q == 7) & b, 0.0, moved)
    return jnp.where(q >= 8 - by // 2, 0.0, roll_rows(x, -(by // 2)))


def jacobian_rows(u, v, w, h, k):
    return [
        [None, 1.0, None, None, None],
        [0.4 * k - u * u, 1.6 * u, -0.4 * v, -0.4 * w, 0.4],
        [-u * v, v, u, None, None],
        [-u * w, w, None, u, None],
        [u * (0.4 * k - h), h - 0.4 * u * u, -0.4 * u * v, -0.4 * u * w, 1.4 * u],
    ]


def jacobian_times(prm, m):
    u, v, w, h, k = prm
    t = m[1] - u * m[0]
    p = 0.4 * (k * m[0] - u * m[1] - v * m[2] - w * m[3] + m[4])
    return [
        m[1],
        p + u * (m[1] + t),
        v * t + u * m[2],
        w * t + u * m[3],
        u * (p + m[4]) + h * t,
    ]


def row_times_jacobian(g, prm, shift):
    u, v, w, h, k = prm
    e = g[0]
    for value, factor in ((g[1], u), (g[2], v), (g[3], w), (g[4], h)):
        if value is not None:
            e = value * factor if e is None else e + value * factor
    p = g[1] if g[4] is None else g[1] + u * g[4]
    p = 0.4 * p
    s = u + shift

    def part(index, other):
        return other if g[index] is None else s * g[index] + other

    return [
        part(0, k * p - u * e),
        part(1, e - u * p),
        part(2, -(v * p)),
        part(3, -(w * p)),
        part(4, p),
    ]


def scaled(rows, shift, factor):
    out = []
    for r in range(5):
        row = []
        for c in range(5):
            value = rows[r][c]
            if r == c:
                value = shift if value is None else value + shift
            row.append(None if value is None else value * factor)
        out.append(row)
    return out


def plus(a, b):
    if a is None:
        return b
    return a if b is None else a + b


def shifted(prm, m, shift):
    return [a + shift * b for a, b in zip(jacobian_times(prm, m), m)]


def diagonal_rows(left, right, here, before, sigma, after):
    rows = []
    for r in range(5):
        own = row_times_jacobian([plus(left[r][c], right[r][c]) for c in range(5)], here, 0.0)
        for c in range(5):
            if left[r][c] is not None:
                own[c] = own[c] + (after * right[r][c] - before * left[r][c])
        own[r] = own[r] + (1.0 + 2.0 * sigma)
        rows.append(own)
    return rows


def factor_rows(rows):
    rows = list(rows)
    recip = []
    for p in range(5):
        rec = 1.0 / rows[p][p]
        recip.append(rec)
        for r in range(p + 1, 5):
            weight = rows[r][p] * rec
            tail = rows[r][p + 1 :] - weight[None] * rows[p][p + 1 :] if p < 4 else None
            parts = [rows[r][:p], weight[None], tail] if p else [weight[None], tail]
            rows[r] = jnp.concatenate(parts, axis=0)
    return rows, recip


def solve_rows(lu, recip, right):
    x = list(right)
    for p in range(5):
        for r in range(p + 1, 5):
            x[r] = x[r] - lu[r][p] * x[p]
    for p in range(4, -1, -1):
        x[p] = x[p] * recip[p]
        for r in range(p):
            x[r] = x[r] - lu[r][p] * x[p]
    return x


def identity(like):
    one, zero = jnp.ones_like(like), jnp.zeros_like(like)
    return [jnp.stack([one if r == c else zero for c in range(5)]) for r in range(5)]


def inverse_of(rows):
    return solve_rows(*factor_rows(rows), identity(rows[0][0]))


def normalise(d_ref, x_ref, s):
    rows = [d_ref[s, r] for r in range(5)]
    unit = identity(rows[0][0])
    x = solve_rows(*factor_rows(rows), [jnp.concatenate([x_ref[s, r], unit[r]], axis=0) for r in range(5)])
    for r in range(5):
        x_ref[s, r], d_ref[s, r] = x[r][:10], x[r][10:]


def times(rows, m):
    return [row_times(row, m) for row in rows]


def row_times(row, others):
    first = row[0] * others[0] + row[1] * others[1]
    return first + (row[2] * others[2] + row[3] * others[3]) + row[4] * others[4]


def combine(own, diagonal, before, after, d_ref, x_ref, s):
    for r in range(5):
        left = row_times(own[r][:5], before)
        right = row_times(own[r][5:], after)
        d_ref[s, r] = diagonal[r] - left[5:] - right[:5]
        x_ref[s, r] = jnp.concatenate([-left[:5], -right[5:]], axis=0)


def subtract(own, r, before, after):
    return r - (row_times(own[:5], before) + row_times(own[5:], after))


def kernel(
    state_ref, visc_ref, resid_ref, out_ref,
    st, vis, res, ro, halo, away, gg, send_m, recv_m, send_r, recv_r, send_x, recv_x,
    prm, d1, l1, d2, l2, dp, lp,
    in_sem, halo_send, halo_recv, a2a_send, a2a_recv, own_sem,
):
    me = lax.axis_index("stream")
    z = lax.axis_index("normal")
    z_count = lax.axis_size("normal")

    def load(k, source, target):
        return pltpu.make_async_copy(source, target, in_sem.at[k])

    loads = [
        load(0, state_ref, st.at[:, :, pl.ds(8, 16), :]),
        load(1, visc_ref, vis),
        load(2, resid_ref, res),
    ]
    for each in loads:
        each.start()

    halo[...] = jnp.zeros_like(halo)
    has_up, has_down = z < z_count - 1, z > 0
    along_x = [lax.rem(me // 8 + d, 4) * 8 for d in range(4)]
    along_y = [lax.rem(lax.rem(me // 2, 4) + d, 4) * 2 for d in range(4)]
    cores = [lax.rem(me, 2), 1 - lax.rem(me, 2)]
    steps = [(dx, dy, dc) for dx in range(4) for dy in range(4) for dc in (1, 0) if dx or dy or dc]
    steps.sort(key=lambda d: -(min(d[0], 4 - d[0]) + min(d[1], 4 - d[1])))

    def for_partners(action):
        for dx, dy, dc in steps:
            action(along_x[dx] + along_y[dy] + cores[dc])

    barrier = pltpu.get_barrier_semaphore()

    @pl.when(has_up)
    def _():
        pl.semaphore_signal(barrier, inc=1, device_id={"normal": z + 1}, device_id_type=MESH)

    @pl.when(has_down)
    def _():
        pl.semaphore_signal(barrier, inc=1, device_id={"normal": z - 1}, device_id_type=MESH)

    for_partners(lambda t: pl.semaphore_signal(barrier, inc=1, device_id={"stream": t}, device_id_type=MESH))
    for ends in (pl.ds(0, 8), pl.ds(24, 8)):
        st[:, :, ends, :] = jnp.zeros((5, 4, 8, 128), jnp.float32)
        gg[:, ends, :] = jnp.zeros((5, 8, 128), jnp.float32)

    slot = lax.rem(me + N - 4, N)

    def message(buf, which, t):
        return buf.at[pl.ds(pl.multiple_of(t * R, R), ROWS[which])]

    def slot_of(t):
        return lax.rem(t + N - 4, N)

    def there(send, recv, which, t):
        if which == 2:
            return message(send, which, t), message(recv, which, slot)
        return message(send, which, slot_of(t)), message(recv, which, me)

    def own_copy(send, recv, which):
        return pltpu.make_async_copy(*there(send, recv, which, me), own_sem.at[which])

    def send_to(send, recv, which, t):
        source, target = there(send, recv, which, t)
        pltpu.make_async_remote_copy(
            src_ref=source, dst_ref=target,
            send_sem=a2a_send.at[which], recv_sem=a2a_recv.at[which],
            device_id={"stream": t}, device_id_type=MESH,
        ).start()

    def exchange(send, recv, which):
        for_partners(lambda t: send_to(send, recv, which, t))
        own_copy(send, recv, which).start()

    def all_of(send, recv, which):
        return pltpu.make_async_remote_copy(
            src_ref=send.at[pl.ds(0, (N - 1) * ROWS[which])], dst_ref=recv.at[pl.ds(0, (N - 1) * ROWS[which])],
            send_sem=a2a_send.at[which], recv_sem=a2a_recv.at[which],
            device_id={"stream": lax.rem(me + 1, N)}, device_id_type=MESH,
        )

    def arrived(send, recv, which):
        all_of(send, recv, which).wait_recv()
        own_copy(send, recv, which).wait()

    def put(send, row, a, b):
        for h, rows in enumerate(swap_halves(a, b)):
            send[pl.ds(h * R + row, 16, stride=2 * R), :] = rows

    loads[0].wait()
    loads[1].wait()
    for p in range(5):
        for cell in range(4):
            away[0, p, cell] = st[p, cell, pl.ds(22, 2), :]
            away[1, p, cell] = st[p, cell, pl.ds(8, 2), :]
    gas_own, sig = [], [vis[cell] for cell in range(4)]
    for cell in range(4):
        rho, m1, m2, m3, energy = (st[p, cell, pl.ds(8, 16), :] for p in range(5))
        inverse = 1.0 / rho
        u, v, w = m1 * inverse, m2 * inverse, m3 * inverse
        k = 0.5 * (u * u + v * v + w * w)
        gas_own.append((u, v, w, 1.4 * energy * inverse - 0.4 * k, k))
    for c in range(2):
        for p in range(4):
            put(send_m, 2 * p + c, gas_own[c][p], gas_own[c + 2][p])
        put(send_m, 8 + c, sig[c], sig[c + 2])

    pl.semaphore_wait(barrier, N - 1 + has_up.astype(jnp.int32) + has_down.astype(jnp.int32))
    upward = pltpu.make_async_remote_copy(
        src_ref=away.at[0], dst_ref=halo.at[0],
        send_sem=halo_send.at[0], recv_sem=halo_recv.at[0],
        device_id={"normal": lax.rem(z + 1, z_count)}, device_id_type=MESH,
    )
    downward = pltpu.make_async_remote_copy(
        src_ref=away.at[1], dst_ref=halo.at[1],
        send_sem=halo_send.at[1], recv_sem=halo_recv.at[1],
        device_id={"normal": lax.rem(z + z_count - 1, z_count)}, device_id_type=MESH,
    )
    pl.when(has_up)(upward.start)
    pl.when(has_down)(downward.start)
    exchange(send_m, recv_m, 0)

    def flux_of(q):
        rho, m1, m2, m3, energy = q
        inverse = 1.0 / rho
        pressure = 0.4 * (energy - 0.5 * (m1 * m1 + m2 * m2 + m3 * m3) * inverse)
        v = m2 * inverse
        return [m2, m1 * v, m2 * v + pressure, m3 * v, (energy + pressure) * v]

    loads[2].wait()
    for cell in range(4):
        flux = flux_of([st[p, cell, pl.ds(8, 16), :] for p in range(5)])
        for p in range(5):
            gg[p, pl.ds(8, 16)] = flux[p]
            s = {d: st[p, cell, pl.ds(8 + d, 16), :] for d in (-2, -1, 0, 1, 2)}
            g = {d: gg[p, pl.ds(8 + d, 16), :] for d in (-1, 1)}
            ro[cell, p] = (
                res[p, cell]
                - 40.0 * (g[1] - g[-1])
                + vis[cell] * (s[1] - 2.0 * s[0] + s[-1])
                - 8.0 * (s[2] - 4.0 * s[1] + 6.0 * s[0] - 4.0 * s[-1] + s[-2])
            )

    inv1, inv3 = (1.0 / (1.0 + 2.0 * sig[cell]) for cell in (1, 3))
    own_inverse = inverse_of([
        jnp.stack(values)
        for values in diagonal_rows(
            scaled(jacobian_rows(*gas_own[1]), sig[2], inv1), scaled(jacobian_rows(*gas_own[3]), -sig[2], inv3),
            gas_own[2], sig[1], sig[2], sig[3],
        )
    ])

    def around(y1, x2, y3):
        flux = jacobian_times(gas_own[2], x2)
        x1 = [y1[p] - inv1 * (flux[p] - sig[1] * x2[p]) for p in range(5)]
        return x1, [y3[p] + inv3 * (flux[p] + sig[3] * x2[p]) for p in range(5)]

    def to_cell_2(y1, y3):
        a, b = shifted(gas_own[1], y1, sig[2]), shifted(gas_own[3], y3, -sig[2])
        return [a[p] - b[p] for p in range(5)]

    def condensed():
        y1, y3 = [inv1 * ro[1, p] for p in range(5)], [inv3 * ro[3, p] for p in range(5)]
        t = to_cell_2(y1, y3)
        x2 = times(own_inverse, [ro[2, p] + t[p] for p in range(5)])
        x1, x3 = around(y1, x2, y3)
        t = shifted(gas_own[1], x1, -sig[0])
        return [ro[0, p] - t[p] for p in range(5)], x3, y1, x2, y3

    rest, x3, *_ = condensed()
    for p in range(5):
        put(send_r, p, rest[p], x3[p])

    def inner(t):
        @pl.when(t >= 8)
        def _():
            send_to(send_r, recv_r, 1, t)

    for_partners(inner)

    pl.when(has_down)(upward.wait_recv)
    pl.when(has_up)(downward.wait_recv)
    index = lax.broadcasted_iota(jnp.int32, (8, 128), 0)
    low = index < 4
    edge = (index == 0) | (index == 7)

    def inward(plane):
        return jnp.where(low, roll_rows(plane, -1), roll_rows(plane, 1))

    for cell in range(4):
        between = jnp.zeros((4, 128), jnp.float32)
        q = [jnp.concatenate([halo[0, p, cell], between, halo[1, p, cell]], axis=0) for p in range(5)]
        flux = flux_of([jnp.where(q[0] > 0.0, q[0], 1.0)] + q[1:])
        factor = 32.0 + jnp.where(low, vis[cell, pl.ds(0, 8), :], vis[cell, pl.ds(8, 8), :])
        for p in range(5):
            change = jnp.where(edge, factor * inward(q[p]) + jnp.where(low, 40.0, -40.0) * inward(flux[p]), 0.0)
            change = change - 8.0 * q[p]
            ro[cell, p, pl.ds(0, 8), :] = ro[cell, p, pl.ds(0, 8), :] + jnp.where(low, change, 0.0)
            ro[cell, p, pl.ds(8, 8), :] = ro[cell, p, pl.ds(8, 8), :] + jnp.where(low, 0.0, change)
    rest, x3, y1, x2, y3 = condensed()
    for p in range(5):
        for h, rows in enumerate(swap_halves(rest[p], x3[p])):
            for end in range(2):
                send_r[pl.ds((28 * end + h) * R + p, 2, stride=2 * R), :] = rows[14 * end : 14 * end + 2]

    def outer(t):
        @pl.when(t != me)
        def _():
            send_to(send_r, recv_r, 1, t)

    for dy in (2, 1, 3, 0):
        for dc in (1, 0):
            outer(along_y[dy] + cores[dc])
    own_copy(send_r, recv_r, 1).start()

    def get(recv, row, e):
        return swap_halves(*(recv[pl.ds((2 * b + e) * R + row, 8, stride=4 * R), :] for b in range(2)))

    arrived(send_m, recv_m, 0)
    for e in range(2):
        for c in range(2):
            both = [get(recv_m, 2 * p + c, e) for p in range(5)]
            for side in range(2):
                u, v, w, h, sigma = (both[p][side] for p in range(5))
                k = 0.5 * (u * u + v * v + w * w)
                cell = 4 * e + c + 2 * side
                values = (u, v, w, h, k, sigma, 1.0 / (1.0 + 2.0 * sigma))
                for p in range(7):
                    prm[p, cell + 2] = values[p]
                    if cell >= 6:
                        prm[p, cell - 6] = previous(values[p], 1)
                    if cell == 0:
                        prm[p, 10] = following(values[p], 1)

    def gas(place_):
        return tuple(prm[p, place_] for p in range(5))

    def level_1(i, carry):
        at = 2 * i + 2
        sigma, before, after = prm[5, at], prm[5, at - 1], prm[5, at + 1]
        left = scaled(jacobian_rows(*gas(at - 1)), sigma, prm[6, at - 1])
        right = scaled(jacobian_rows(*gas(at + 1)), -sigma, prm[6, at + 1])
        here, far_left, far_right = gas(at), gas(at - 2), gas(at + 2)
        own = diagonal_rows(left, right, here, before, sigma, after)
        for r in range(5):
            lower = row_times_jacobian(left[r], far_left, before)
            upper = row_times_jacobian(right[r], far_right, -after)
            for c in range(5):
                d1[i + 1, r, c] = own[r][c]
                l1[i + 1, r, c] = -lower[c]
                l1[i + 1, r, 5 + c] = -upper[c]
        return carry

    for i in range(4):
        level_1(i, 0)

    def level_2_normalise(i, carry):
        normalise(d1, l1, 2 * i + 2)
        return carry

    for i in range(2):
        level_2_normalise(i, 0)
    for r in range(5):
        l1[0, r] = previous(l1[4, r], 1)

    def rows_of(ref, s):
        return [ref[s, r] for r in range(5)]

    def level_2_combine(i, carry):
        s = 2 * i + 1
        combine(rows_of(l1, s), rows_of(d1, s), rows_of(l1, s - 1), rows_of(l1, s + 1), d2, l2, i)
        return carry

    for i in range(2):
        level_2_combine(i, 0)

    normalise(d2, l2, 1)
    combine(
        rows_of(l2, 0), rows_of(d2, 0), [previous(l2[1, r], 1) for r in range(5)], rows_of(l2, 1), dp, lp, 0
    )

    unit = identity(jnp.ones((8, 128), jnp.float32))
    for step in range(3):
        normalise(dp, lp, step)
        own = rows_of(lp, step)
        combine(
            own, unit, [previous(x, 2**step) for x in own], [following(x, 2**step) for x in own],
            dp, lp, step + 1,
        )
    q, _ = place((5, 8, 128))
    other = [jnp.where(q < 4, lp[3, r, pl.ds(5, 5)], lp[3, r, pl.ds(0, 5)]) for r in range(5)]
    both = solve_rows(*factor_rows(rows_of(dp, 3)), [jnp.concatenate([other[r], unit[r]], axis=0) for r in range(5)])
    other, fourth = [row[:5] for row in both], [row[5:] for row in both]
    facing = [roll_rows(x, 4) for x in other]
    last = inverse_of([unit[r] - row_times(other[r], facing) for r in range(5)])

    arrived(send_r, recv_r, 1)
    parts = [[get(recv_r, p, e) for p in range(5)] for e in range(2)]
    inside = [[parts[e][p][1] for p in range(5)] for e in range(2)]
    four = {}
    for i, before in ((0, [previous(value, 1) for value in inside[1]]), (4, inside[0])):
        t = shifted(gas(i + 1), before, prm[5, i + 2])
        four[i] = [parts[i // 4][p][0] + t[p] for p in range(5)]
    y = {}
    y[4] = times(rows_of(d2, 1), four[4])
    before = [previous(value, 1) for value in y[4]]
    b = [subtract(l2[0, r], four[0][r], before, y[4]) for r in range(5)]
    for step in range(3):
        b = times(rows_of(dp, step), b)
        before = [previous(value, 2**step) for value in b]
        after = [following(value, 2**step) for value in b]
        b = [subtract(lp[step, r], b[r], before, after) for r in range(5)]
    b = times(fourth, b)
    paired = [roll_rows(value, 4) for value in b]
    b = [b[r] - row_times(other[r], paired) for r in range(5)]
    x = {0: times(last, b)}
    x[8] = [following(value, 1) for value in x[0]]
    x[4] = [subtract(l2[1, r], y[4][r], x[0], x[8]) for r in range(5)]

    for e in range(2):
        beyond = shifted(gas(4 * e + 6), x[4 * e + 4], -prm[5, 4 * e + 5])
        for p in range(5):
            for b, rows in enumerate(swap_halves(x[4 * e][p], beyond[p])):
                send_x[pl.ds((2 * b + e) * R + p, 8, stride=4 * R), :] = rows
    exchange(send_x, recv_x, 2)
    arrived(send_x, recv_x, 2)
    both = [swap_halves(*(recv_x[pl.ds(h * R + p, 16, stride=2 * R), :] for h in range(2))) for p in range(5)]
    x0 = [both[p][0] for p in range(5)]
    after = [inv3 * both[p][1] for p in range(5)]
    before = [inv1 * value for value in shifted(gas_own[0], x0, sig[1])]
    t = times(own_inverse, to_cell_2(before, [-value for value in after]))
    x2 = [x2[p] + t[p] for p in range(5)]
    x1, x3 = around([y1[p] + before[p] for p in range(5)], x2, [y3[p] - after[p] for p in range(5)])
    for p in range(5):
        out_ref[p, 0], out_ref[p, 1], out_ref[p, 2], out_ref[p, 3] = x0[p], x1[p], x2[p], x3[p]

    pl.when(has_up)(upward.wait_send)
    pl.when(has_down)(downward.wait_send)
    for which, (send, recv) in enumerate(((send_m, recv_m), (send_r, recv_r), (send_x, recv_x))):
        all_of(send, recv, which).wait_send()


def on_device(state, viscosity, residual_other):
    f32 = jnp.float32
    tile = (8, 128)
    buffer = pltpu.VMEM((N * R, 128), f32)
    return pl.pallas_call(
        kernel,
        out_shape=jax.ShapeDtypeStruct(state.shape, f32),
        in_specs=[pl.BlockSpec(memory_space=pltpu.HBM)] * 3,
        out_specs=pl.BlockSpec(memory_space=pltpu.VMEM),
        scratch_shapes=[
            pltpu.VMEM((5, 4, 32, 128), f32),
            pltpu.VMEM((4, 16, 128), f32),
            pltpu.VMEM((5, 4, 16, 128), f32),
            pltpu.VMEM((4, 5, 16, 128), f32),
            pltpu.VMEM((2, 5, 4, 2, 128), f32),
            pltpu.VMEM((2, 5, 4, 2, 128), f32),
            pltpu.VMEM((5, 32, 128), f32),
        ]
        + [buffer, buffer, pltpu.VMEM((3 * N * R // 2, 128), f32), buffer, buffer, buffer]
        + [
            pltpu.VMEM((7, 11) + tile, f32),
            pltpu.VMEM((5, 5, 5) + tile, f32),
            pltpu.VMEM((5, 5, 10) + tile, f32),
            pltpu.VMEM((2, 5, 5) + tile, f32),
            pltpu.VMEM((2, 5, 10) + tile, f32),
            pltpu.VMEM((4, 5, 5) + tile, f32),
            pltpu.VMEM((4, 5, 10) + tile, f32),
            pltpu.SemaphoreType.DMA((3,)),
            pltpu.SemaphoreType.DMA((2,)),
            pltpu.SemaphoreType.DMA((2,)),
            pltpu.SemaphoreType.DMA((3,)),
            pltpu.SemaphoreType.DMA((3,)),
            pltpu.SemaphoreType.DMA((3,)),
        ],
        compiler_params=pltpu.CompilerParams(
            collective_id=0, has_side_effects=True, vmem_limit_bytes=32 * 1024 * 1024
        ),
    )(*(pltpu.with_memory_space_constraint(x, pltpu.HBM) for x in (state, viscosity, residual_other)))


def solution(mesh):
    placed = (
        P(None, "stream", "normal", None),
        P("stream", "normal", None),
        P(None, "stream", "normal", None),
    )
    return jax.shard_map(
        on_device,
        mesh=mesh,
        in_specs=placed,
        out_specs=P(None, "stream", "normal", None),
        check_vma=False,
    )
```

```python
import jax
import jax.numpy as jnp
from jax import lax
from jax.experimental import pallas as pl
from jax.experimental.pallas import tpu as pltpu
from jax.sharding import PartitionSpec as P

N = 32
R = 16
ROWS = (10, 5, 5)
HALF = 64
MESH = pl.DeviceIdType.MESH


def roll_lanes(x):
    return pltpu.roll(x, HALF, axis=x.ndim - 1)


def roll_rows(x, by):
    return pltpu.roll(x, by % 8, axis=x.ndim - 2)


def swap_halves(a, b):
    low = lax.broadcasted_iota(jnp.int32, a.shape, a.ndim - 1) < HALF
    return jnp.where(low, a, roll_lanes(b)), jnp.where(low, roll_lanes(a), b)


def place(shape):
    q = lax.broadcasted_iota(jnp.int32, shape, len(shape) - 2)
    b = lax.broadcasted_iota(jnp.int32, shape, len(shape) - 1) >= HALF
    return q, b


def previous(x, by):
    q, b = place(x.shape)
    if by == 1:
        moved = roll_lanes(jnp.where(b, roll_rows(x, 1), x))
        return jnp.where((q == 0) & ~b, 0.0, moved)
    return jnp.where(q < by // 2, 0.0, roll_rows(x, by // 2))


def following(x, by):
    q, b = place(x.shape)
    if by == 1:
        moved = roll_lanes(jnp.where(b, x, roll_rows(x, -1)))
        return jnp.where((q == 7) & b, 0.0, moved)
    return jnp.where(q >= 8 - by // 2, 0.0, roll_rows(x, -(by // 2)))


def jacobian_rows(u, v, w, h, k):
    return [
        [None, 1.0, None, None, None],
        [0.4 * k - u * u, 1.6 * u, -0.4 * v, -0.4 * w, 0.4],
        [-u * v, v, u, None, None],
        [-u * w, w, None, u, None],
        [u * (0.4 * k - h), h - 0.4 * u * u, -0.4 * u * v, -0.4 * u * w, 1.4 * u],
    ]


def jacobian_times(prm, m):
    u, v, w, h, k = prm
    t = m[1] - u * m[0]
    p = 0.4 * (k * m[0] - u * m[1] - v * m[2] - w * m[3] + m[4])
    return [
        m[1],
        p + u * (m[1] + t),
        v * t + u * m[2],
        w * t + u * m[3],
        u * (p + m[4]) + h * t,
    ]


def row_times_jacobian(g, prm, shift):
    u, v, w, h, k = prm
    e = g[0]
    for value, factor in ((g[1], u), (g[2], v), (g[3], w), (g[4], h)):
        if value is not None:
            e = value * factor if e is None else e + value * factor
    p = g[1] if g[4] is None else g[1] + u * g[4]
    p = 0.4 * p
    s = u + shift

    def part(index, other):
        return other if g[index] is None else s * g[index] + other

    return [
        part(0, k * p - u * e),
        part(1, e - u * p),
        part(2, -(v * p)),
        part(3, -(w * p)),
        part(4, p),
    ]


def scaled(rows, shift, factor):
    out = []
    for r in range(5):
        row = []
        for c in range(5):
            value = rows[r][c]
            if r == c:
                value = shift if value is None else value + shift
            row.append(None if value is None else value * factor)
        out.append(row)
    return out


def plus(a, b):
    if a is None:
        return b
    return a if b is None else a + b


def shifted(prm, m, shift):
    return [a + shift * b for a, b in zip(jacobian_times(prm, m), m)]


def diagonal_rows(left, right, here, before, sigma, after):
    rows = []
    for r in range(5):
        own = row_times_jacobian([plus(left[r][c], right[r][c]) for c in range(5)], here, 0.0)
        for c in range(5):
            if left[r][c] is not None:
                own[c] = own[c] + (after * right[r][c] - before * left[r][c])
        own[r] = own[r] + (1.0 + 2.0 * sigma)
        rows.append(own)
    return rows


def factor_rows(rows):
    rows = list(rows)
    recip = []
    for p in range(5):
        rec = 1.0 / rows[p][p]
        recip.append(rec)
        for r in range(p + 1, 5):
            weight = rows[r][p] * rec
            tail = rows[r][p + 1 :] - weight[None] * rows[p][p + 1 :] if p < 4 else None
            parts = [rows[r][:p], weight[None], tail] if p else [weight[None], tail]
            rows[r] = jnp.concatenate(parts, axis=0)
    return rows, recip


def solve_rows(lu, recip, right):
    x = list(right)
    for p in range(5):
        for r in range(p + 1, 5):
            x[r] = x[r] - lu[r][p] * x[p]
    for p in range(4, -1, -1):
        x[p] = x[p] * recip[p]
        for r in range(p):
            x[r] = x[r] - lu[r][p] * x[p]
    return x


def identity(like):
    one, zero = jnp.ones_like(like), jnp.zeros_like(like)
    return [jnp.stack([one if r == c else zero for c in range(5)]) for r in range(5)]


def inverse_of(rows):
    return solve_rows(*factor_rows(rows), identity(rows[0][0]))


def normalise(d_ref, x_ref, s, keep=True):
    rows = [d_ref[s, r] for r in range(5)]
    unit = identity(rows[0][0])
    right = [jnp.concatenate([x_ref[s, r], unit[r]], axis=0) if keep else x_ref[s, r] for r in range(5)]
    x = solve_rows(*factor_rows(rows), right)
    for r in range(5):
        x_ref[s, r] = x[r][:10]
        if keep:
            d_ref[s, r] = x[r][10:]


def times(rows, m):
    return [row_times(row, m) for row in rows]


def row_times(row, others):
    first = row[0] * others[0] + row[1] * others[1]
    return first + (row[2] * others[2] + row[3] * others[3]) + row[4] * others[4]


def combine(own, diagonal, before, after, d_ref, x_ref, s):
    for r in range(5):
        left = row_times(own[r][:5], before)
        right = row_times(own[r][5:], after)
        d_ref[s, r] = diagonal[r] - left[5:] - right[:5]
        x_ref[s, r] = jnp.concatenate([-left[:5], -right[5:]], axis=0)


def subtract(own, r, before, after):
    return r - (row_times(own[:5], before) + row_times(own[5:], after))


def kernel(
    state_ref, visc_ref, resid_ref, out_ref,
    st, vis, res, ro, halo, away, gg, send_m, recv_m, send_r, recv_r, send_x, recv_x,
    prm, d1, l1, d2, l2, dp, lp,
    in_sem, halo_send, halo_recv, a2a_send, a2a_recv, own_sem,
):
    me = lax.axis_index("stream")
    z = lax.axis_index("normal")
    z_count = lax.axis_size("normal")

    has_up, has_down = z < z_count - 1, z > 0
    along_x = [lax.rem(me // 8 + d, 4) * 8 for d in range(4)]
    along_y = [lax.rem(lax.rem(me // 2, 4) + d, 4) * 2 for d in range(4)]
    cores = [lax.rem(me, 2), 1 - lax.rem(me, 2)]
    steps = [(dx, dy, dc) for dx in range(4) for dy in range(4) for dc in (1, 0) if dx or dy or dc]
    steps.sort(key=lambda d: -(min(d[0], 4 - d[0]) + min(d[1], 4 - d[1])))

    def for_partners(action, first=0, last=N):
        for dx, dy, dc in steps[first:last]:
            action(along_x[dx] + along_y[dy] + cores[dc])

    barrier = pltpu.get_barrier_semaphore()

    def greet(t):
        pl.semaphore_signal(barrier, inc=1, device_id={"stream": t}, device_id_type=MESH)

    for_partners(greet, 0, 10)
    def load(k, source, target):
        return pltpu.make_async_copy(source, target, in_sem.at[k])

    loads = [
        load(0, state_ref, st.at[:, :, pl.ds(8, 16), :]),
        load(1, visc_ref, vis),
        load(2, resid_ref, res),
    ]
    for each in loads:
        each.start()

    halo[...] = jnp.zeros_like(halo)
    @pl.when(has_up)
    def _():
        pl.semaphore_signal(barrier, inc=1, device_id={"normal": z + 1}, device_id_type=MESH)

    @pl.when(has_down)
    def _():
        pl.semaphore_signal(barrier, inc=1, device_id={"normal": z - 1}, device_id_type=MESH)

    for_partners(greet, 10)
    for ends in (pl.ds(0, 8), pl.ds(24, 8)):
        st[:, :, ends, :] = jnp.zeros((5, 4, 8, 128), jnp.float32)
        gg[:, ends, :] = jnp.zeros((5, 8, 128), jnp.float32)

    slot = lax.rem(me + N - 4, N)

    def message(buf, which, t):
        return buf.at[pl.ds(pl.multiple_of(t * R, R), ROWS[which])]

    def slot_of(t):
        return lax.rem(t + N - 4, N)

    def there(send, recv, which, t):
        if which == 2:
            return message(send, which, t), message(recv, which, slot)
        return message(send, which, slot_of(t)), message(recv, which, me)

    def own_copy(send, recv, which):
        return pltpu.make_async_copy(*there(send, recv, which, me), own_sem.at[which])

    def send_to(send, recv, which, t):
        source, target = there(send, recv, which, t)
        pltpu.make_async_remote_copy(
            src_ref=source, dst_ref=target,
            send_sem=a2a_send.at[which], recv_sem=a2a_recv.at[which],
            device_id={"stream": t}, device_id_type=MESH,
        ).start()

    def exchange(send, recv, which):
        for_partners(lambda t: send_to(send, recv, which, t))
        own_copy(send, recv, which).start()

    def all_of(send, recv, which):
        return pltpu.make_async_remote_copy(
            src_ref=send.at[pl.ds(0, (N - 1) * ROWS[which])], dst_ref=recv.at[pl.ds(0, (N - 1) * ROWS[which])],
            send_sem=a2a_send.at[which], recv_sem=a2a_recv.at[which],
            device_id={"stream": lax.rem(me + 1, N)}, device_id_type=MESH,
        )

    def arrived(send, recv, which):
        all_of(send, recv, which).wait_recv()
        own_copy(send, recv, which).wait()

    def put(send, row, a, b):
        for h, rows in enumerate(swap_halves(a, b)):
            send[pl.ds(h * R + row, 16, stride=2 * R), :] = rows

    loads[0].wait()
    loads[1].wait()
    for p in range(5):
        for cell in range(4):
            away[0, p, cell] = st[p, cell, pl.ds(22, 2), :]
            away[1, p, cell] = st[p, cell, pl.ds(8, 2), :]
    gas_own, sig = [], [vis[cell] for cell in range(4)]
    for cell in range(4):
        rho, m1, m2, m3, energy = (st[p, cell, pl.ds(8, 16), :] for p in range(5))
        inverse = 1.0 / rho
        u, v, w = m1 * inverse, m2 * inverse, m3 * inverse
        k = 0.5 * (u * u + v * v + w * w)
        gas_own.append((u, v, w, 1.4 * energy * inverse - 0.4 * k, k))
    for c in range(2):
        for p in range(4):
            put(send_m, 2 * p + c, gas_own[c][p], gas_own[c + 2][p])
        put(send_m, 8 + c, sig[c], sig[c + 2])

    pl.semaphore_wait(barrier, N - 1 + has_up.astype(jnp.int32) + has_down.astype(jnp.int32))
    upward = pltpu.make_async_remote_copy(
        src_ref=away.at[0], dst_ref=halo.at[0],
        send_sem=halo_send.at[0], recv_sem=halo_recv.at[0],
        device_id={"normal": lax.rem(z + 1, z_count)}, device_id_type=MESH,
    )
    downward = pltpu.make_async_remote_copy(
        src_ref=away.at[1], dst_ref=halo.at[1],
        send_sem=halo_send.at[1], recv_sem=halo_recv.at[1],
        device_id={"normal": lax.rem(z + z_count - 1, z_count)}, device_id_type=MESH,
    )
    pl.when(has_up)(upward.start)
    pl.when(has_down)(downward.start)
    exchange(send_m, recv_m, 0)

    def flux_of(q):
        rho, m1, m2, m3, energy = q
        inverse = 1.0 / rho
        pressure = 0.4 * (energy - 0.5 * (m1 * m1 + m2 * m2 + m3 * m3) * inverse)
        v = m2 * inverse
        return [m2, m1 * v, m2 * v + pressure, m3 * v, (energy + pressure) * v]

    loads[2].wait()
    for cell in range(4):
        flux = flux_of([st[p, cell, pl.ds(8, 16), :] for p in range(5)])
        for p in range(5):
            gg[p, pl.ds(8, 16)] = flux[p]
            s = {d: st[p, cell, pl.ds(8 + d, 16), :] for d in (-2, -1, 0, 1, 2)}
            g = {d: gg[p, pl.ds(8 + d, 16), :] for d in (-1, 1)}
            ro[cell, p] = (
                res[p, cell]
                - 40.0 * (g[1] - g[-1])
                + vis[cell] * (s[1] - 2.0 * s[0] + s[-1])
                - 8.0 * (s[2] - 4.0 * s[1] + 6.0 * s[0] - 4.0 * s[-1] + s[-2])
            )

    inv1, inv3 = (1.0 / (1.0 + 2.0 * sig[cell]) for cell in (1, 3))
    own_inverse = inverse_of([
        jnp.stack(values)
        for values in diagonal_rows(
            scaled(jacobian_rows(*gas_own[1]), sig[2], inv1), scaled(jacobian_rows(*gas_own[3]), -sig[2], inv3),
            gas_own[2], sig[1], sig[2], sig[3],
        )
    ])

    def around(y1, x2, y3):
        flux = jacobian_times(gas_own[2], x2)
        x1 = [y1[p] - inv1 * (flux[p] - sig[1] * x2[p]) for p in range(5)]
        return x1, [y3[p] + inv3 * (flux[p] + sig[3] * x2[p]) for p in range(5)]

    def to_cell_2(y1, y3):
        a, b = shifted(gas_own[1], y1, sig[2]), shifted(gas_own[3], y3, -sig[2])
        return [a[p] - b[p] for p in range(5)]

    def condensed():
        y1, y3 = [inv1 * ro[1, p] for p in range(5)], [inv3 * ro[3, p] for p in range(5)]
        t = to_cell_2(y1, y3)
        x2 = times(own_inverse, [ro[2, p] + t[p] for p in range(5)])
        x1, x3 = around(y1, x2, y3)
        t = shifted(gas_own[1], x1, -sig[0])
        return [ro[0, p] - t[p] for p in range(5)], x3, y1, x2, y3

    rest, x3, *_ = condensed()
    for p in range(5):
        put(send_r, p, rest[p], x3[p])

    def inner(t):
        @pl.when(t >= 8)
        def _():
            send_to(send_r, recv_r, 1, t)

    for_partners(inner)

    pl.when(has_down)(upward.wait_recv)
    pl.when(has_up)(downward.wait_recv)
    index = lax.broadcasted_iota(jnp.int32, (8, 128), 0)
    low = index < 4
    edge = (index == 0) | (index == 7)

    def inward(plane):
        return jnp.where(low, roll_rows(plane, -1), roll_rows(plane, 1))

    for cell in range(4):
        between = jnp.zeros((4, 128), jnp.float32)
        q = [jnp.concatenate([halo[0, p, cell], between, halo[1, p, cell]], axis=0) for p in range(5)]
        flux = flux_of([jnp.where(q[0] > 0.0, q[0], 1.0)] + q[1:])
        factor = 32.0 + jnp.where(low, vis[cell, pl.ds(0, 8), :], vis[cell, pl.ds(8, 8), :])
        for p in range(5):
            change = jnp.where(edge, factor * inward(q[p]) + jnp.where(low, 40.0, -40.0) * inward(flux[p]), 0.0)
            change = change - 8.0 * q[p]
            ro[cell, p, pl.ds(0, 8), :] = ro[cell, p, pl.ds(0, 8), :] + jnp.where(low, change, 0.0)
            ro[cell, p, pl.ds(8, 8), :] = ro[cell, p, pl.ds(8, 8), :] + jnp.where(low, 0.0, change)
    rest, x3, y1, x2, y3 = condensed()
    for p in range(5):
        for h, rows in enumerate(swap_halves(rest[p], x3[p])):
            for end in range(2):
                send_r[pl.ds((28 * end + h) * R + p, 2, stride=2 * R), :] = rows[14 * end : 14 * end + 2]

    def outer(t):
        @pl.when(t != me)
        def _():
            send_to(send_r, recv_r, 1, t)

    for dy in (2, 1, 3, 0):
        for dc in (1, 0):
            outer(along_y[dy] + cores[dc])
    own_copy(send_r, recv_r, 1).start()

    def get(recv, row, e):
        return swap_halves(*(recv[pl.ds((2 * b + e) * R + row, 8, stride=4 * R), :] for b in range(2)))

    arrived(send_m, recv_m, 0)
    for e in range(2):
        for c in range(2):
            both = [get(recv_m, 2 * p + c, e) for p in range(5)]
            for side in range(2):
                u, v, w, h, sigma = (both[p][side] for p in range(5))
                k = 0.5 * (u * u + v * v + w * w)
                cell = 4 * e + c + 2 * side
                values = (u, v, w, h, k, sigma, 1.0 / (1.0 + 2.0 * sigma))
                for p in range(7):
                    prm[p, cell + 2] = values[p]
                    if cell >= 6:
                        prm[p, cell - 6] = previous(values[p], 1)
                    if cell == 0:
                        prm[p, 10] = following(values[p], 1)

    def gas(place_):
        return tuple(prm[p, place_] for p in range(5))

    def level_1(i, carry):
        at = 2 * i + 2
        sigma, before, after = prm[5, at], prm[5, at - 1], prm[5, at + 1]
        left = scaled(jacobian_rows(*gas(at - 1)), sigma, prm[6, at - 1])
        right = scaled(jacobian_rows(*gas(at + 1)), -sigma, prm[6, at + 1])
        here, far_left, far_right = gas(at), gas(at - 2), gas(at + 2)
        own = diagonal_rows(left, right, here, before, sigma, after)
        for r in range(5):
            lower = row_times_jacobian(left[r], far_left, before)
            upper = row_times_jacobian(right[r], far_right, -after)
            for c in range(5):
                d1[i + 1, r, c] = own[r][c]
                l1[i + 1, r, c] = -lower[c]
                l1[i + 1, r, 5 + c] = -upper[c]
        return carry

    for i in range(4):
        level_1(i, 0)

    def level_2_normalise(i, carry):
        normalise(d1, l1, 2 * i + 2, keep=False)
        return carry

    for i in range(2):
        level_2_normalise(i, 0)
    for r in range(5):
        l1[0, r] = previous(l1[4, r], 1)

    def rows_of(ref, s):
        return [ref[s, r] for r in range(5)]

    def level_2_combine(i, carry):
        s = 2 * i + 1
        combine(rows_of(l1, s), rows_of(d1, s), rows_of(l1, s - 1), rows_of(l1, s + 1), d2, l2, i)
        return carry

    for i in range(2):
        level_2_combine(i, 0)

    normalise(d2, l2, 1)
    combine(
        rows_of(l2, 0), rows_of(d2, 0), [previous(l2[1, r], 1) for r in range(5)], rows_of(l2, 1), dp, lp, 0
    )

    unit = identity(jnp.ones((8, 128), jnp.float32))
    for step in range(3):
        normalise(dp, lp, step)
        own = rows_of(lp, step)
        combine(
            own, unit, [previous(x, 2**step) for x in own], [following(x, 2**step) for x in own],
            dp, lp, step + 1,
        )
    q, _ = place((5, 8, 128))
    other = [jnp.where(q < 4, lp[3, r, pl.ds(5, 5)], lp[3, r, pl.ds(0, 5)]) for r in range(5)]
    both = solve_rows(*factor_rows(rows_of(dp, 3)), [jnp.concatenate([other[r], unit[r]], axis=0) for r in range(5)])
    other, fourth = [row[:5] for row in both], [row[5:] for row in both]
    facing = [roll_rows(x, 4) for x in other]
    last = inverse_of([unit[r] - row_times(other[r], facing) for r in range(5)])

    arrived(send_r, recv_r, 1)
    parts = [[get(recv_r, p, e) for p in range(5)] for e in range(2)]
    inside = [[parts[e][p][1] for p in range(5)] for e in range(2)]
    four = {}
    for i, before in ((0, [previous(value, 1) for value in inside[1]]), (4, inside[0])):
        t = shifted(gas(i + 1), before, prm[5, i + 2])
        four[i] = [parts[i // 4][p][0] + t[p] for p in range(5)]
    y = {}
    y[4] = times(rows_of(d2, 1), four[4])
    before = [previous(value, 1) for value in y[4]]
    b = [subtract(l2[0, r], four[0][r], before, y[4]) for r in range(5)]
    for step in range(3):
        b = times(rows_of(dp, step), b)
        before = [previous(value, 2**step) for value in b]
        after = [following(value, 2**step) for value in b]
        b = [subtract(lp[step, r], b[r], before, after) for r in range(5)]
    b = times(fourth, b)
    paired = [roll_rows(value, 4) for value in b]
    b = [b[r] - row_times(other[r], paired) for r in range(5)]
    x = {0: times(last, b)}
    x[8] = [following(value, 1) for value in x[0]]
    x[4] = [subtract(l2[1, r], y[4][r], x[0], x[8]) for r in range(5)]

    for e in range(2):
        beyond = shifted(gas(4 * e + 6), x[4 * e + 4], -prm[5, 4 * e + 5])
        for p in range(5):
            for b, rows in enumerate(swap_halves(x[4 * e][p], beyond[p])):
                send_x[pl.ds((2 * b + e) * R + p, 8, stride=4 * R), :] = rows
    exchange(send_x, recv_x, 2)
    arrived(send_x, recv_x, 2)
    both = [swap_halves(*(recv_x[pl.ds(h * R + p, 16, stride=2 * R), :] for h in range(2))) for p in range(5)]
    x0 = [both[p][0] for p in range(5)]
    after = [inv3 * both[p][1] for p in range(5)]
    before = [inv1 * value for value in shifted(gas_own[0], x0, sig[1])]
    t = times(own_inverse, to_cell_2(before, [-value for value in after]))
    x2 = [x2[p] + t[p] for p in range(5)]
    x1, x3 = around([y1[p] + before[p] for p in range(5)], x2, [y3[p] - after[p] for p in range(5)])
    for p in range(5):
        out_ref[p, 0], out_ref[p, 1], out_ref[p, 2], out_ref[p, 3] = x0[p], x1[p], x2[p], x3[p]

    pl.when(has_up)(upward.wait_send)
    pl.when(has_down)(downward.wait_send)
    for which, (send, recv) in enumerate(((send_m, recv_m), (send_r, recv_r), (send_x, recv_x))):
        all_of(send, recv, which).wait_send()


def on_device(state, viscosity, residual_other):
    f32 = jnp.float32
    tile = (8, 128)
    buffer = pltpu.VMEM((N * R, 128), f32)
    return pl.pallas_call(
        kernel,
        out_shape=jax.ShapeDtypeStruct(state.shape, f32),
        in_specs=[pl.BlockSpec(memory_space=pltpu.HBM)] * 3,
        out_specs=pl.BlockSpec(memory_space=pltpu.VMEM),
        scratch_shapes=[
            pltpu.VMEM((5, 4, 32, 128), f32),
            pltpu.VMEM((4, 16, 128), f32),
            pltpu.VMEM((5, 4, 16, 128), f32),
            pltpu.VMEM((4, 5, 16, 128), f32),
            pltpu.VMEM((2, 5, 4, 2, 128), f32),
            pltpu.VMEM((2, 5, 4, 2, 128), f32),
            pltpu.VMEM((5, 32, 128), f32),
        ]
        + [buffer, buffer, pltpu.VMEM((3 * N * R // 2, 128), f32), buffer, buffer, buffer]
        + [
            pltpu.VMEM((7, 11) + tile, f32),
            pltpu.VMEM((5, 5, 5) + tile, f32),
            pltpu.VMEM((5, 5, 10) + tile, f32),
            pltpu.VMEM((2, 5, 5) + tile, f32),
            pltpu.VMEM((2, 5, 10) + tile, f32),
            pltpu.VMEM((4, 5, 5) + tile, f32),
            pltpu.VMEM((4, 5, 10) + tile, f32),
            pltpu.SemaphoreType.DMA((3,)),
            pltpu.SemaphoreType.DMA((2,)),
            pltpu.SemaphoreType.DMA((2,)),
            pltpu.SemaphoreType.DMA((3,)),
            pltpu.SemaphoreType.DMA((3,)),
            pltpu.SemaphoreType.DMA((3,)),
        ],
        compiler_params=pltpu.CompilerParams(
            collective_id=0, has_side_effects=True, vmem_limit_bytes=32 * 1024 * 1024
        ),
    )(*(pltpu.with_memory_space_constraint(x, pltpu.HBM) for x in (state, viscosity, residual_other)))


def solution(mesh):
    placed = (
        P(None, "stream", "normal", None),
        P("stream", "normal", None),
        P(None, "stream", "normal", None),
    )
    return jax.shard_map(
        on_device,
        mesh=mesh,
        in_specs=placed,
        out_specs=P(None, "stream", "normal", None),
        check_vma=False,
    )
```

```python
import jax
import jax.numpy as jnp
from jax import lax
from jax.experimental import pallas as pl
from jax.experimental.pallas import tpu as pltpu
from jax.sharding import PartitionSpec as P

N = 32
R = 16
ROWS = (10, 5, 5)
HALF = 64
MESH = pl.DeviceIdType.MESH


def roll_lanes(x):
    return pltpu.roll(x, HALF, axis=x.ndim - 1)


def roll_rows(x, by):
    return pltpu.roll(x, by % 8, axis=x.ndim - 2)


def swap_halves(a, b):
    low = lax.broadcasted_iota(jnp.int32, a.shape, a.ndim - 1) < HALF
    return jnp.where(low, a, roll_lanes(b)), jnp.where(low, roll_lanes(a), b)


def place(shape):
    q = lax.broadcasted_iota(jnp.int32, shape, len(shape) - 2)
    b = lax.broadcasted_iota(jnp.int32, shape, len(shape) - 1) >= HALF
    return q, b


def previous(x, by):
    q, b = place(x.shape)
    if by == 1:
        other = roll_lanes(x)
        return jnp.where(b, other, jnp.where(q == 0, 0.0, roll_rows(other, 1)))
    return jnp.where(q < by // 2, 0.0, roll_rows(x, by // 2))


def following(x, by):
    q, b = place(x.shape)
    if by == 1:
        other = roll_lanes(x)
        return jnp.where(b, jnp.where(q == 7, 0.0, roll_rows(other, -1)), other)
    return jnp.where(q >= 8 - by // 2, 0.0, roll_rows(x, -(by // 2)))


def jacobian_rows(u, v, w, h, k):
    return [
        [None, 1.0, None, None, None],
        [0.4 * k - u * u, 1.6 * u, -0.4 * v, -0.4 * w, 0.4],
        [-u * v, v, u, None, None],
        [-u * w, w, None, u, None],
        [u * (0.4 * k - h), h - 0.4 * u * u, -0.4 * u * v, -0.4 * u * w, 1.4 * u],
    ]


def jacobian_times(prm, m):
    u, v, w, h, k = prm
    t = m[1] - u * m[0]
    p = 0.4 * (k * m[0] - u * m[1] - v * m[2] - w * m[3] + m[4])
    return [
        m[1],
        p + u * (m[1] + t),
        v * t + u * m[2],
        w * t + u * m[3],
        u * (p + m[4]) + h * t,
    ]


def row_times_jacobian(g, prm, shift):
    u, v, w, h, k = prm
    e = g[0]
    for value, factor in ((g[1], u), (g[2], v), (g[3], w), (g[4], h)):
        if value is not None:
            e = value * factor if e is None else e + value * factor
    p = g[1] if g[4] is None else g[1] + u * g[4]
    p = 0.4 * p
    s = u + shift

    def part(index, other):
        return other if g[index] is None else s * g[index] + other

    return [
        part(0, k * p - u * e),
        part(1, e - u * p),
        part(2, -(v * p)),
        part(3, -(w * p)),
        part(4, p),
    ]


def scaled(rows, shift, factor):
    out = []
    for r in range(5):
        row = []
        for c in range(5):
            value = rows[r][c]
            if r == c:
                value = shift if value is None else value + shift
            row.append(None if value is None else value * factor)
        out.append(row)
    return out


def plus(a, b):
    if a is None:
        return b
    return a if b is None else a + b


def shifted(prm, m, shift):
    return [a + shift * b for a, b in zip(jacobian_times(prm, m), m)]


def diagonal_rows(left, right, here, before, sigma, after):
    rows = []
    for r in range(5):
        own = row_times_jacobian([plus(left[r][c], right[r][c]) for c in range(5)], here, 0.0)
        for c in range(5):
            if left[r][c] is not None:
                own[c] = own[c] + (after * right[r][c] - before * left[r][c])
        own[r] = own[r] + (1.0 + 2.0 * sigma)
        rows.append(own)
    return rows


def factor_rows(rows):
    rows = list(rows)
    recip = []
    for p in range(5):
        rec = 1.0 / rows[p][p]
        recip.append(rec)
        for r in range(p + 1, 5):
            weight = rows[r][p] * rec
            tail = rows[r][p + 1 :] - weight[None] * rows[p][p + 1 :] if p < 4 else None
            parts = [rows[r][:p], weight[None], tail] if p else [weight[None], tail]
            rows[r] = jnp.concatenate(parts, axis=0)
    return rows, recip


def solve_rows(lu, recip, right):
    x = list(right)
    for p in range(5):
        for r in range(p + 1, 5):
            x[r] = x[r] - lu[r][p] * x[p]
    for p in range(4, -1, -1):
        x[p] = x[p] * recip[p]
        for r in range(p):
            x[r] = x[r] - lu[r][p] * x[p]
    return x


def identity(like):
    one, zero = jnp.ones_like(like), jnp.zeros_like(like)
    return [jnp.stack([one if r == c else zero for c in range(5)]) for r in range(5)]


def inverse_of(rows):
    return solve_rows(*factor_rows(rows), identity(rows[0][0]))


def normalise(d_ref, x_ref, s, keep=True):
    rows = [d_ref[s, r] for r in range(5)]
    unit = identity(rows[0][0])
    right = [jnp.concatenate([x_ref[s, r], unit[r]], axis=0) if keep else x_ref[s, r] for r in range(5)]
    x = solve_rows(*factor_rows(rows), right)
    for r in range(5):
        x_ref[s, r] = x[r][:10]
        if keep:
            d_ref[s, r] = x[r][10:]


def times(rows, m):
    return [row_times(row, m) for row in rows]


def row_times(row, others):
    first = row[0] * others[0] + row[1] * others[1]
    return first + (row[2] * others[2] + row[3] * others[3]) + row[4] * others[4]


def combine(own, diagonal, before, after, d_ref, x_ref, s):
    for r in range(5):
        left = row_times(own[r][:5], before)
        right = row_times(own[r][5:], after)
        d_ref[s, r] = diagonal[r] - left[5:] - right[:5]
        x_ref[s, r] = jnp.concatenate([-left[:5], -right[5:]], axis=0)


def subtract(own, r, before, after):
    return r - (row_times(own[:5], before) + row_times(own[5:], after))


def kernel(
    state_ref, visc_ref, resid_ref, out_ref,
    st, vis, res, ro, halo, away, gg, send_m, recv_m, send_r, recv_r, send_x, recv_x,
    prm, d1, l1, d2, l2, dp, lp,
    in_sem, halo_send, halo_recv, a2a_send, a2a_recv, own_sem,
):
    me = lax.axis_index("stream")
    z = lax.axis_index("normal")
    z_count = lax.axis_size("normal")

    has_up, has_down = z < z_count - 1, z > 0
    along_x = [lax.rem(me // 8 + d, 4) * 8 for d in range(4)]
    along_y = [lax.rem(lax.rem(me // 2, 4) + d, 4) * 2 for d in range(4)]
    cores = [lax.rem(me, 2), 1 - lax.rem(me, 2)]
    steps = [(dx, dy, dc) for dx in range(4) for dy in range(4) for dc in (1, 0) if dx or dy or dc]
    steps.sort(key=lambda d: -(min(d[0], 4 - d[0]) + min(d[1], 4 - d[1])))

    def for_partners(action, first=0, last=N):
        for dx, dy, dc in steps[first:last]:
            action(along_x[dx] + along_y[dy] + cores[dc])

    barrier = pltpu.get_barrier_semaphore()

    def greet(t):
        pl.semaphore_signal(barrier, inc=1, device_id={"stream": t}, device_id_type=MESH)

    for_partners(greet, 0, 10)
    def load(k, source, target):
        return pltpu.make_async_copy(source, target, in_sem.at[k])

    loads = [
        load(0, state_ref, st.at[:, :, pl.ds(8, 16), :]),
        load(1, visc_ref, vis),
        load(2, resid_ref, res),
    ]
    for each in loads:
        each.start()

    halo[pl.ds(0, 2)] = jnp.zeros((2, 5, 4, 2, 128), jnp.float32)
    @pl.when(has_up)
    def _():
        pl.semaphore_signal(barrier, inc=1, device_id={"normal": z + 1}, device_id_type=MESH)

    @pl.when(has_down)
    def _():
        pl.semaphore_signal(barrier, inc=1, device_id={"normal": z - 1}, device_id_type=MESH)

    for_partners(greet, 10)
    for ends in (pl.ds(0, 8), pl.ds(24, 8)):
        st[:, :, ends, :] = jnp.zeros((5, 4, 8, 128), jnp.float32)
        gg[:, ends, :] = jnp.zeros((5, 8, 128), jnp.float32)

    slot = lax.rem(me + N - 4, N)

    def message(buf, which, t):
        return buf.at[pl.ds(pl.multiple_of(t * R, R), ROWS[which])]

    def slot_of(t):
        return lax.rem(t + N - 4, N)

    def there(send, recv, which, t):
        if which == 2:
            return message(send, which, t), message(recv, which, slot)
        return message(send, which, slot_of(t)), message(recv, which, me)

    def own_copy(send, recv, which):
        return pltpu.make_async_copy(*there(send, recv, which, me), own_sem.at[which])

    def send_to(send, recv, which, t):
        source, target = there(send, recv, which, t)
        pltpu.make_async_remote_copy(
            src_ref=source, dst_ref=target,
            send_sem=a2a_send.at[which], recv_sem=a2a_recv.at[which],
            device_id={"stream": t}, device_id_type=MESH,
        ).start()

    def exchange(send, recv, which):
        for_partners(lambda t: send_to(send, recv, which, t))
        own_copy(send, recv, which).start()

    def all_of(send, recv, which):
        return pltpu.make_async_remote_copy(
            src_ref=send.at[pl.ds(0, (N - 1) * ROWS[which])], dst_ref=recv.at[pl.ds(0, (N - 1) * ROWS[which])],
            send_sem=a2a_send.at[which], recv_sem=a2a_recv.at[which],
            device_id={"stream": lax.rem(me + 1, N)}, device_id_type=MESH,
        )

    def arrived(send, recv, which):
        all_of(send, recv, which).wait_recv()
        own_copy(send, recv, which).wait()

    def put(send, row, a, b):
        for h, rows in enumerate(swap_halves(a, b)):
            send[pl.ds(h * R + row, 16, stride=2 * R), :] = rows

    loads[0].wait()
    loads[1].wait()
    for p in range(5):
        for cell in range(4):
            away[0, p, cell] = st[p, cell, pl.ds(22, 2), :]
            away[1, p, cell] = st[p, cell, pl.ds(8, 2), :]
    gas_own, sig = [], [vis[cell] for cell in range(4)]
    for cell in range(4):
        rho, m1, m2, m3, energy = (st[p, cell, pl.ds(8, 16), :] for p in range(5))
        inverse = 1.0 / rho
        u, v, w = m1 * inverse, m2 * inverse, m3 * inverse
        k = 0.5 * (u * u + v * v + w * w)
        gas_own.append((u, v, w, 1.4 * energy * inverse - 0.4 * k, k))
    for c in range(2):
        for p in range(4):
            put(send_m, 2 * p + c, gas_own[c][p], gas_own[c + 2][p])
        put(send_m, 8 + c, sig[c], sig[c + 2])

    pl.semaphore_wait(barrier, N - 1 + has_up.astype(jnp.int32) + has_down.astype(jnp.int32))
    upward = pltpu.make_async_remote_copy(
        src_ref=away.at[0], dst_ref=halo.at[0],
        send_sem=halo_send.at[0], recv_sem=halo_recv.at[0],
        device_id={"normal": lax.rem(z + 1, z_count)}, device_id_type=MESH,
    )
    downward = pltpu.make_async_remote_copy(
        src_ref=away.at[1], dst_ref=halo.at[1],
        send_sem=halo_send.at[1], recv_sem=halo_recv.at[1],
        device_id={"normal": lax.rem(z + z_count - 1, z_count)}, device_id_type=MESH,
    )
    pl.when(has_up)(upward.start)
    pl.when(has_down)(downward.start)
    exchange(send_m, recv_m, 0)

    def flux_of(q):
        rho, m1, m2, m3, energy = q
        inverse = 1.0 / rho
        pressure = 0.4 * (energy - 0.5 * (m1 * m1 + m2 * m2 + m3 * m3) * inverse)
        v = m2 * inverse
        return [m2, m1 * v, m2 * v + pressure, m3 * v, (energy + pressure) * v]

    loads[2].wait()
    for cell in range(4):
        flux = flux_of([st[p, cell, pl.ds(8, 16), :] for p in range(5)])
        for p in range(5):
            gg[p, pl.ds(8, 16)] = flux[p]
            s = {d: st[p, cell, pl.ds(8 + d, 16), :] for d in (-2, -1, 0, 1, 2)}
            g = {d: gg[p, pl.ds(8 + d, 16), :] for d in (-1, 1)}
            ro[cell, p] = (
                res[p, cell]
                - 40.0 * (g[1] - g[-1])
                + vis[cell] * (s[1] - 2.0 * s[0] + s[-1])
                - 8.0 * (s[2] - 4.0 * s[1] + 6.0 * s[0] - 4.0 * s[-1] + s[-2])
            )

    inv1, inv3 = (1.0 / (1.0 + 2.0 * sig[cell]) for cell in (1, 3))
    own_inverse = inverse_of([
        jnp.stack(values)
        for values in diagonal_rows(
            scaled(jacobian_rows(*gas_own[1]), sig[2], inv1), scaled(jacobian_rows(*gas_own[3]), -sig[2], inv3),
            gas_own[2], sig[1], sig[2], sig[3],
        )
    ])

    def around(y1, x2, y3):
        flux = jacobian_times(gas_own[2], x2)
        x1 = [y1[p] - inv1 * (flux[p] - sig[1] * x2[p]) for p in range(5)]
        return x1, [y3[p] + inv3 * (flux[p] + sig[3] * x2[p]) for p in range(5)]

    def to_cell_2(y1, y3):
        a, b = shifted(gas_own[1], y1, sig[2]), shifted(gas_own[3], y3, -sig[2])
        return [a[p] - b[p] for p in range(5)]

    def condensed():
        y1, y3 = [inv1 * ro[1, p] for p in range(5)], [inv3 * ro[3, p] for p in range(5)]
        t = to_cell_2(y1, y3)
        x2 = times(own_inverse, [ro[2, p] + t[p] for p in range(5)])
        x1, x3 = around(y1, x2, y3)
        t = shifted(gas_own[1], x1, -sig[0])
        return [ro[0, p] - t[p] for p in range(5)], x3, y1, x2, y3

    rest, x3, *_ = condensed()
    for p in range(5):
        put(send_r, p, rest[p], x3[p])

    def inner(t):
        @pl.when(t >= 8)
        def _():
            send_to(send_r, recv_r, 1, t)

    for_partners(inner)

    pl.when(has_down)(upward.wait_recv)
    pl.when(has_up)(downward.wait_recv)
    index = lax.broadcasted_iota(jnp.int32, (8, 128), 0)
    low = index < 4
    edge = (index == 0) | (index == 7)

    def inward(plane):
        return jnp.where(low, roll_rows(plane, -1), roll_rows(plane, 1))

    for cell in range(4):
        between = jnp.zeros((4, 128), jnp.float32)
        q = [jnp.concatenate([halo[0, p, cell], between, halo[1, p, cell]], axis=0) for p in range(5)]
        flux = flux_of([jnp.where(q[0] > 0.0, q[0], 1.0)] + q[1:])
        factor = 32.0 + jnp.where(low, vis[cell, pl.ds(0, 8), :], vis[cell, pl.ds(8, 8), :])
        for p in range(5):
            change = jnp.where(edge, factor * inward(q[p]) + jnp.where(low, 40.0, -40.0) * inward(flux[p]), 0.0)
            change = change - 8.0 * q[p]
            ro[cell, p, pl.ds(0, 8), :] = ro[cell, p, pl.ds(0, 8), :] + jnp.where(low, change, 0.0)
            ro[cell, p, pl.ds(8, 8), :] = ro[cell, p, pl.ds(8, 8), :] + jnp.where(low, 0.0, change)
    rest, x3, y1, x2, y3 = condensed()
    for p in range(5):
        for h, rows in enumerate(swap_halves(rest[p], x3[p])):
            for end in range(2):
                send_r[pl.ds((28 * end + h) * R + p, 2, stride=2 * R), :] = rows[14 * end : 14 * end + 2]

    def outer(t):
        @pl.when(t != me)
        def _():
            send_to(send_r, recv_r, 1, t)

    for dy in (2, 1, 3, 0):
        for dc in (1, 0):
            outer(along_y[dy] + cores[dc])
    own_copy(send_r, recv_r, 1).start()

    def get(recv, row, e):
        return swap_halves(*(recv[pl.ds((2 * b + e) * R + row, 8, stride=4 * R), :] for b in range(2)))

    arrived(send_m, recv_m, 0)
    for e in range(2):
        for c in range(2):
            both = [get(recv_m, 2 * p + c, e) for p in range(5)]
            for side in range(2):
                u, v, w, h, sigma = (both[p][side] for p in range(5))
                k = 0.5 * (u * u + v * v + w * w)
                cell = 4 * e + c + 2 * side
                values = (u, v, w, h, k, sigma, 1.0 / (1.0 + 2.0 * sigma))
                for p in range(7):
                    prm[p, cell + 2] = values[p]
                    if cell >= 6:
                        prm[p, cell - 6] = previous(values[p], 1)
                    if cell == 0:
                        prm[p, 10] = following(values[p], 1)

    def gas(place_):
        return tuple(prm[p, place_] for p in range(5))

    def level_1(i, carry):
        at = 2 * i + 2
        sigma, before, after = prm[5, at], prm[5, at - 1], prm[5, at + 1]
        left = scaled(jacobian_rows(*gas(at - 1)), sigma, prm[6, at - 1])
        right = scaled(jacobian_rows(*gas(at + 1)), -sigma, prm[6, at + 1])
        here, far_left, far_right = gas(at), gas(at - 2), gas(at + 2)
        own = diagonal_rows(left, right, here, before, sigma, after)
        for r in range(5):
            lower = row_times_jacobian(left[r], far_left, before)
            upper = row_times_jacobian(right[r], far_right, -after)
            for c in range(5):
                d1[i + 1, r, c] = own[r][c]
                l1[i + 1, r, c] = -lower[c]
                l1[i + 1, r, 5 + c] = -upper[c]
        return carry

    for i in range(4):
        level_1(i, 0)

    def level_2_normalise(i, carry):
        normalise(d1, l1, 2 * i + 2, keep=False)
        return carry

    for i in range(2):
        level_2_normalise(i, 0)
    for r in range(5):
        l1[0, r] = previous(l1[4, r], 1)

    def rows_of(ref, s):
        return [ref[s, r] for r in range(5)]

    def level_2_combine(i, carry):
        s = 2 * i + 1
        combine(rows_of(l1, s), rows_of(d1, s), rows_of(l1, s - 1), rows_of(l1, s + 1), d2, l2, i)
        return carry

    for i in range(2):
        level_2_combine(i, 0)

    normalise(d2, l2, 1)
    combine(
        rows_of(l2, 0), rows_of(d2, 0), [previous(l2[1, r], 1) for r in range(5)], rows_of(l2, 1), dp, lp, 0
    )

    unit = identity(jnp.ones((8, 128), jnp.float32))
    for step in range(3):
        normalise(dp, lp, step)
        own = rows_of(lp, step)
        combine(
            own, unit, [previous(x, 2**step) for x in own], [following(x, 2**step) for x in own],
            dp, lp, step + 1,
        )
    q, _ = place((5, 8, 128))
    other = [jnp.where(q < 4, lp[3, r, pl.ds(5, 5)], lp[3, r, pl.ds(0, 5)]) for r in range(5)]
    both = solve_rows(*factor_rows(rows_of(dp, 3)), [jnp.concatenate([other[r], unit[r]], axis=0) for r in range(5)])
    other, fourth = [row[:5] for row in both], [row[5:] for row in both]
    facing = [roll_rows(x, 4) for x in other]
    last = inverse_of([unit[r] - row_times(other[r], facing) for r in range(5)])

    arrived(send_r, recv_r, 1)
    parts = [[get(recv_r, p, e) for p in range(5)] for e in range(2)]
    inside = [[parts[e][p][1] for p in range(5)] for e in range(2)]
    four = {}
    for i, before in ((0, [previous(value, 1) for value in inside[1]]), (4, inside[0])):
        t = shifted(gas(i + 1), before, prm[5, i + 2])
        four[i] = [parts[i // 4][p][0] + t[p] for p in range(5)]
    y = {}
    y[4] = times(rows_of(d2, 1), four[4])
    before = [previous(value, 1) for value in y[4]]
    b = [subtract(l2[0, r], four[0][r], before, y[4]) for r in range(5)]
    for step in range(3):
        b = times(rows_of(dp, step), b)
        before = [previous(value, 2**step) for value in b]
        after = [following(value, 2**step) for value in b]
        b = [subtract(lp[step, r], b[r], before, after) for r in range(5)]
    b = times(fourth, b)
    paired = [roll_rows(value, 4) for value in b]
    b = [b[r] - row_times(other[r], paired) for r in range(5)]
    x = {0: times(last, b)}
    x[8] = [following(value, 1) for value in x[0]]
    x[4] = [subtract(l2[1, r], y[4][r], x[0], x[8]) for r in range(5)]

    for e in range(2):
        beyond = shifted(gas(4 * e + 6), x[4 * e + 4], -prm[5, 4 * e + 5])
        for p in range(5):
            for b, rows in enumerate(swap_halves(x[4 * e][p], beyond[p])):
                send_x[pl.ds((2 * b + e) * R + p, 8, stride=4 * R), :] = rows
    exchange(send_x, recv_x, 2)
    arrived(send_x, recv_x, 2)
    both = [swap_halves(*(recv_x[pl.ds(h * R + p, 16, stride=2 * R), :] for h in range(2))) for p in range(5)]
    x0 = [both[p][0] for p in range(5)]
    after = [inv3 * both[p][1] for p in range(5)]
    before = [inv1 * value for value in shifted(gas_own[0], x0, sig[1])]
    t = times(own_inverse, to_cell_2(before, [-value for value in after]))
    x2 = [x2[p] + t[p] for p in range(5)]
    x1, x3 = around([y1[p] + before[p] for p in range(5)], x2, [y3[p] - after[p] for p in range(5)])
    for p in range(5):
        out_ref[p, 0], out_ref[p, 1], out_ref[p, 2], out_ref[p, 3] = x0[p], x1[p], x2[p], x3[p]

    pl.when(has_up)(upward.wait_send)
    pl.when(has_down)(downward.wait_send)
    for which, (send, recv) in enumerate(((send_m, recv_m), (send_r, recv_r), (send_x, recv_x))):
        all_of(send, recv, which).wait_send()


def on_device(state, viscosity, residual_other):
    f32 = jnp.float32
    tile = (8, 128)
    buffer = pltpu.VMEM((N * R, 128), f32)
    return pl.pallas_call(
        kernel,
        out_shape=jax.ShapeDtypeStruct(state.shape, f32),
        in_specs=[pl.BlockSpec(memory_space=pltpu.HBM)] * 3,
        out_specs=pl.BlockSpec(memory_space=pltpu.VMEM),
        scratch_shapes=[
            pltpu.VMEM((5, 4, 32, 128), f32),
            pltpu.VMEM((4, 16, 128), f32),
            pltpu.VMEM((5, 4, 16, 128), f32),
            pltpu.VMEM((4, 5, 16, 128), f32),
            pltpu.VMEM((3, 5, 4, 2, 128), f32),
            pltpu.VMEM((3, 5, 4, 2, 128), f32),
            pltpu.VMEM((5, 32, 128), f32),
        ]
        + [buffer, buffer, pltpu.VMEM((3 * N * R // 2, 128), f32), buffer, buffer, buffer]
        + [
            pltpu.VMEM((7, 11) + tile, f32),
            pltpu.VMEM((5, 5, 5) + tile, f32),
            pltpu.VMEM((5, 5, 10) + tile, f32),
            pltpu.VMEM((2, 5, 5) + tile, f32),
            pltpu.VMEM((2, 5, 10) + tile, f32),
            pltpu.VMEM((4, 5, 5) + tile, f32),
            pltpu.VMEM((4, 5, 10) + tile, f32),
            pltpu.SemaphoreType.DMA((3,)),
            pltpu.SemaphoreType.DMA((2,)),
            pltpu.SemaphoreType.DMA((2,)),
            pltpu.SemaphoreType.DMA((3,)),
            pltpu.SemaphoreType.DMA((3,)),
            pltpu.SemaphoreType.DMA((3,)),
        ],
        compiler_params=pltpu.CompilerParams(
            collective_id=0, has_side_effects=True, vmem_limit_bytes=32 * 1024 * 1024
        ),
    )(*(pltpu.with_memory_space_constraint(x, pltpu.HBM) for x in (state, viscosity, residual_other)))


def solution(mesh):
    placed = (
        P(None, "stream", "normal", None),
        P("stream", "normal", None),
        P(None, "stream", "normal", None),
    )
    return jax.shard_map(
        on_device,
        mesh=mesh,
        in_specs=placed,
        out_specs=P(None, "stream", "normal", None),
        check_vma=False,
    )
```

```python
import jax
import jax.numpy as jnp
from jax import lax
from jax.experimental import pallas as pl
from jax.experimental.pallas import tpu as pltpu
from jax.sharding import PartitionSpec as P

N = 32
R = 16
ROWS = (10, 5, 5)
HALF = 64
MESH = pl.DeviceIdType.MESH


def roll_lanes(x):
    return pltpu.roll(x, HALF, axis=x.ndim - 1)


def roll_rows(x, by):
    return pltpu.roll(x, by % 8, axis=x.ndim - 2)


def swap_halves(a, b):
    low = lax.broadcasted_iota(jnp.int32, a.shape, a.ndim - 1) < HALF
    return jnp.where(low, a, roll_lanes(b)), jnp.where(low, roll_lanes(a), b)


def place(shape):
    q = lax.broadcasted_iota(jnp.int32, shape, len(shape) - 2)
    b = lax.broadcasted_iota(jnp.int32, shape, len(shape) - 1) >= HALF
    return q, b


def previous(x, by):
    q, b = place(x.shape)
    if by == 1:
        other = roll_lanes(x)
        return jnp.where(b, other, jnp.where(q == 0, 0.0, roll_rows(other, 1)))
    return jnp.where(q < by // 2, 0.0, roll_rows(x, by // 2))


def following(x, by):
    q, b = place(x.shape)
    if by == 1:
        other = roll_lanes(x)
        return jnp.where(b, jnp.where(q == 7, 0.0, roll_rows(other, -1)), other)
    return jnp.where(q >= 8 - by // 2, 0.0, roll_rows(x, -(by // 2)))


def jacobian_rows(u, v, w, h, k):
    return [
        [None, 1.0, None, None, None],
        [0.4 * k - u * u, 1.6 * u, -0.4 * v, -0.4 * w, 0.4],
        [-u * v, v, u, None, None],
        [-u * w, w, None, u, None],
        [u * (0.4 * k - h), h - 0.4 * u * u, -0.4 * u * v, -0.4 * u * w, 1.4 * u],
    ]


def jacobian_times(prm, m):
    u, v, w, h, k = prm
    t = m[1] - u * m[0]
    p = 0.4 * (k * m[0] - u * m[1] - v * m[2] - w * m[3] + m[4])
    return [
        m[1],
        p + u * (m[1] + t),
        v * t + u * m[2],
        w * t + u * m[3],
        u * (p + m[4]) + h * t,
    ]


def row_times_jacobian(g, prm, shift):
    u, v, w, h, k = prm
    e = g[0]
    for value, factor in ((g[1], u), (g[2], v), (g[3], w), (g[4], h)):
        if value is not None:
            e = value * factor if e is None else e + value * factor
    p = g[1] if g[4] is None else g[1] + u * g[4]
    p = 0.4 * p
    s = u + shift

    def part(index, other):
        return other if g[index] is None else s * g[index] + other

    return [
        part(0, k * p - u * e),
        part(1, e - u * p),
        part(2, -(v * p)),
        part(3, -(w * p)),
        part(4, p),
    ]


def scaled(rows, shift, factor):
    out = []
    for r in range(5):
        row = []
        for c in range(5):
            value = rows[r][c]
            if r == c:
                value = shift if value is None else value + shift
            row.append(None if value is None else value * factor)
        out.append(row)
    return out


def plus(a, b):
    if a is None:
        return b
    return a if b is None else a + b


def shifted(prm, m, shift):
    return [a + shift * b for a, b in zip(jacobian_times(prm, m), m)]


def diagonal_rows(left, right, here, before, sigma, after):
    rows = []
    for r in range(5):
        own = row_times_jacobian([plus(left[r][c], right[r][c]) for c in range(5)], here, 0.0)
        for c in range(5):
            if left[r][c] is not None:
                own[c] = own[c] + (after * right[r][c] - before * left[r][c])
        own[r] = own[r] + (1.0 + 2.0 * sigma)
        rows.append(own)
    return rows


def factor_rows(rows):
    rows = list(rows)
    recip = []
    for p in range(5):
        rec = 1.0 / rows[p][p]
        recip.append(rec)
        for r in range(p + 1, 5):
            weight = rows[r][p] * rec
            tail = rows[r][p + 1 :] - weight[None] * rows[p][p + 1 :] if p < 4 else None
            parts = [rows[r][:p], weight[None], tail] if p else [weight[None], tail]
            rows[r] = jnp.concatenate(parts, axis=0)
    return rows, recip


def solve_rows(lu, recip, right):
    x = list(right)
    for p in range(5):
        for r in range(p + 1, 5):
            x[r] = x[r] - lu[r][p] * x[p]
    for p in range(4, -1, -1):
        x[p] = x[p] * recip[p]
        for r in range(p):
            x[r] = x[r] - lu[r][p] * x[p]
    return x


def identity(like):
    one, zero = jnp.ones_like(like), jnp.zeros_like(like)
    return [jnp.stack([one if r == c else zero for c in range(5)]) for r in range(5)]


def inverse_of(rows):
    return solve_rows(*factor_rows(rows), identity(rows[0][0]))


def normalise(d_ref, x_ref, s, keep=True):
    rows = [d_ref[s, r] for r in range(5)]
    unit = identity(rows[0][0])
    right = [jnp.concatenate([x_ref[s, r], unit[r]], axis=0) if keep else x_ref[s, r] for r in range(5)]
    x = solve_rows(*factor_rows(rows), right)
    for r in range(5):
        x_ref[s, r] = x[r][:10]
        if keep:
            d_ref[s, r] = x[r][10:]


def normalised(diagonal, own):
    unit = identity(diagonal[0][0])
    x = solve_rows(*factor_rows(diagonal), [jnp.concatenate([own[r], unit[r]], axis=0) for r in range(5)])
    return [row[10:] for row in x], [row[:10] for row in x]


def combined(own, diagonal, before, after):
    left = [row_times(row[:5], before) for row in own]
    right = [row_times(row[5:], after) for row in own]
    return (
        [diagonal[r] - left[r][5:] - right[r][:5] for r in range(5)],
        [jnp.concatenate([-left[r][:5], -right[r][5:]], axis=0) for r in range(5)],
    )


def times(rows, m):
    return [row_times(row, m) for row in rows]


def row_times(row, others):
    first = row[0] * others[0] + row[1] * others[1]
    return first + (row[2] * others[2] + row[3] * others[3]) + row[4] * others[4]


def combine(own, diagonal, before, after, d_ref, x_ref, s):
    for r in range(5):
        left = row_times(own[r][:5], before)
        right = row_times(own[r][5:], after)
        d_ref[s, r] = diagonal[r] - left[5:] - right[:5]
        x_ref[s, r] = jnp.concatenate([-left[:5], -right[5:]], axis=0)


def subtract(own, r, before, after):
    return r - (row_times(own[:5], before) + row_times(own[5:], after))


def kernel(
    state_ref, visc_ref, resid_ref, out_ref,
    st, vis, res, ro, halo, away, gg, send_m, recv_m, send_r, recv_r, send_x, recv_x,
    prm, d1, l1, d2, l2,
    in_sem, halo_send, halo_recv, a2a_send, a2a_recv, own_sem,
):
    me = lax.axis_index("stream")
    z = lax.axis_index("normal")
    z_count = lax.axis_size("normal")

    has_up, has_down = z < z_count - 1, z > 0
    along_x = [lax.rem(me // 8 + d, 4) * 8 for d in range(4)]
    along_y = [lax.rem(lax.rem(me // 2, 4) + d, 4) * 2 for d in range(4)]
    cores = [lax.rem(me, 2), 1 - lax.rem(me, 2)]
    steps = [(dx, dy, dc) for dx in range(4) for dy in range(4) for dc in (1, 0) if dx or dy or dc]
    steps.sort(key=lambda d: -(min(d[0], 4 - d[0]) + min(d[1], 4 - d[1])))

    def for_partners(action, first=0, last=N):
        for dx, dy, dc in steps[first:last]:
            action(along_x[dx] + along_y[dy] + cores[dc])

    barrier = pltpu.get_barrier_semaphore()

    def greet(t):
        pl.semaphore_signal(barrier, inc=1, device_id={"stream": t}, device_id_type=MESH)

    for_partners(greet, 0, 10)
    def load(k, source, target):
        return pltpu.make_async_copy(source, target, in_sem.at[k])

    loads = [
        load(0, state_ref, st.at[:, :, pl.ds(8, 16), :]),
        load(1, visc_ref, vis),
        load(2, resid_ref, res),
    ]
    for each in loads:
        each.start()

    halo[pl.ds(0, 2)] = jnp.zeros((2, 5, 4, 2, 128), jnp.float32)
    @pl.when(has_up)
    def _():
        pl.semaphore_signal(barrier, inc=1, device_id={"normal": z + 1}, device_id_type=MESH)

    @pl.when(has_down)
    def _():
        pl.semaphore_signal(barrier, inc=1, device_id={"normal": z - 1}, device_id_type=MESH)

    for_partners(greet, 10)
    for ends in (pl.ds(0, 8), pl.ds(24, 8)):
        st[:, :, ends, :] = jnp.zeros((5, 4, 8, 128), jnp.float32)
        gg[:, ends, :] = jnp.zeros((5, 8, 128), jnp.float32)

    slot = lax.rem(me + N - 4, N)

    def message(buf, which, t):
        return buf.at[pl.ds(pl.multiple_of(t * R, R), ROWS[which])]

    def slot_of(t):
        return lax.rem(t + N - 4, N)

    def there(send, recv, which, t):
        if which == 2:
            return message(send, which, t), message(recv, which, slot)
        return message(send, which, slot_of(t)), message(recv, which, me)

    def own_copy(send, recv, which):
        return pltpu.make_async_copy(*there(send, recv, which, me), own_sem.at[which])

    def send_to(send, recv, which, t):
        source, target = there(send, recv, which, t)
        pltpu.make_async_remote_copy(
            src_ref=source, dst_ref=target,
            send_sem=a2a_send.at[which], recv_sem=a2a_recv.at[which],
            device_id={"stream": t}, device_id_type=MESH,
        ).start()

    def exchange(send, recv, which):
        for_partners(lambda t: send_to(send, recv, which, t))
        own_copy(send, recv, which).start()

    def all_of(send, recv, which):
        return pltpu.make_async_remote_copy(
            src_ref=send.at[pl.ds(0, (N - 1) * ROWS[which])], dst_ref=recv.at[pl.ds(0, (N - 1) * ROWS[which])],
            send_sem=a2a_send.at[which], recv_sem=a2a_recv.at[which],
            device_id={"stream": lax.rem(me + 1, N)}, device_id_type=MESH,
        )

    def arrived(send, recv, which):
        all_of(send, recv, which).wait_recv()
        own_copy(send, recv, which).wait()

    def put(send, row, a, b):
        for h, rows in enumerate(swap_halves(a, b)):
            send[pl.ds(h * R + row, 16, stride=2 * R), :] = rows

    loads[0].wait()
    loads[1].wait()
    for p in range(5):
        for cell in range(4):
            away[0, p, cell] = st[p, cell, pl.ds(22, 2), :]
            away[1, p, cell] = st[p, cell, pl.ds(8, 2), :]
    gas_own, sig = [], [vis[cell] for cell in range(4)]
    for cell in range(4):
        rho, m1, m2, m3, energy = (st[p, cell, pl.ds(8, 16), :] for p in range(5))
        inverse = 1.0 / rho
        u, v, w = m1 * inverse, m2 * inverse, m3 * inverse
        k = 0.5 * (u * u + v * v + w * w)
        gas_own.append((u, v, w, 1.4 * energy * inverse - 0.4 * k, k))
    for c in range(2):
        for p in range(4):
            put(send_m, 2 * p + c, gas_own[c][p], gas_own[c + 2][p])
        put(send_m, 8 + c, sig[c], sig[c + 2])

    pl.semaphore_wait(barrier, N - 1 + has_up.astype(jnp.int32) + has_down.astype(jnp.int32))
    upward = pltpu.make_async_remote_copy(
        src_ref=away.at[0], dst_ref=halo.at[0],
        send_sem=halo_send.at[0], recv_sem=halo_recv.at[0],
        device_id={"normal": lax.rem(z + 1, z_count)}, device_id_type=MESH,
    )
    downward = pltpu.make_async_remote_copy(
        src_ref=away.at[1], dst_ref=halo.at[1],
        send_sem=halo_send.at[1], recv_sem=halo_recv.at[1],
        device_id={"normal": lax.rem(z + z_count - 1, z_count)}, device_id_type=MESH,
    )
    pl.when(has_up)(upward.start)
    pl.when(has_down)(downward.start)
    exchange(send_m, recv_m, 0)

    def flux_of(q):
        rho, m1, m2, m3, energy = q
        inverse = 1.0 / rho
        pressure = 0.4 * (energy - 0.5 * (m1 * m1 + m2 * m2 + m3 * m3) * inverse)
        v = m2 * inverse
        return [m2, m1 * v, m2 * v + pressure, m3 * v, (energy + pressure) * v]

    loads[2].wait()
    for cell in range(4):
        flux = flux_of([st[p, cell, pl.ds(8, 16), :] for p in range(5)])
        for p in range(5):
            gg[p, pl.ds(8, 16)] = flux[p]
            s = {d: st[p, cell, pl.ds(8 + d, 16), :] for d in (-2, -1, 0, 1, 2)}
            g = {d: gg[p, pl.ds(8 + d, 16), :] for d in (-1, 1)}
            ro[cell, p] = (
                res[p, cell]
                - 40.0 * (g[1] - g[-1])
                + vis[cell] * (s[1] - 2.0 * s[0] + s[-1])
                - 8.0 * (s[2] - 4.0 * s[1] + 6.0 * s[0] - 4.0 * s[-1] + s[-2])
            )

    inv1, inv3 = (1.0 / (1.0 + 2.0 * sig[cell]) for cell in (1, 3))
    own_inverse = inverse_of([
        jnp.stack(values)
        for values in diagonal_rows(
            scaled(jacobian_rows(*gas_own[1]), sig[2], inv1), scaled(jacobian_rows(*gas_own[3]), -sig[2], inv3),
            gas_own[2], sig[1], sig[2], sig[3],
        )
    ])

    def around(y1, x2, y3):
        flux = jacobian_times(gas_own[2], x2)
        x1 = [y1[p] - inv1 * (flux[p] - sig[1] * x2[p]) for p in range(5)]
        return x1, [y3[p] + inv3 * (flux[p] + sig[3] * x2[p]) for p in range(5)]

    def to_cell_2(y1, y3):
        a, b = shifted(gas_own[1], y1, sig[2]), shifted(gas_own[3], y3, -sig[2])
        return [a[p] - b[p] for p in range(5)]

    def condensed():
        y1, y3 = [inv1 * ro[1, p] for p in range(5)], [inv3 * ro[3, p] for p in range(5)]
        t = to_cell_2(y1, y3)
        x2 = times(own_inverse, [ro[2, p] + t[p] for p in range(5)])
        x1, x3 = around(y1, x2, y3)
        t = shifted(gas_own[1], x1, -sig[0])
        return [ro[0, p] - t[p] for p in range(5)], x3, y1, x2, y3

    rest, x3, *_ = condensed()
    for p in range(5):
        put(send_r, p, rest[p], x3[p])

    def inner(t):
        @pl.when(t >= 8)
        def _():
            send_to(send_r, recv_r, 1, t)

    for_partners(inner)

    pl.when(has_down)(upward.wait_recv)
    pl.when(has_up)(downward.wait_recv)
    index = lax.broadcasted_iota(jnp.int32, (8, 128), 0)
    low = index < 4
    edge = (index == 0) | (index == 7)

    def inward(plane):
        return jnp.where(low, roll_rows(plane, -1), roll_rows(plane, 1))

    for cell in range(4):
        between = jnp.zeros((4, 128), jnp.float32)
        q = [jnp.concatenate([halo[0, p, cell], between, halo[1, p, cell]], axis=0) for p in range(5)]
        flux = flux_of([jnp.where(q[0] > 0.0, q[0], 1.0)] + q[1:])
        factor = 32.0 + jnp.where(low, vis[cell, pl.ds(0, 8), :], vis[cell, pl.ds(8, 8), :])
        for p in range(5):
            change = jnp.where(edge, factor * inward(q[p]) + jnp.where(low, 40.0, -40.0) * inward(flux[p]), 0.0)
            change = change - 8.0 * q[p]
            ro[cell, p, pl.ds(0, 8), :] = ro[cell, p, pl.ds(0, 8), :] + jnp.where(low, change, 0.0)
            ro[cell, p, pl.ds(8, 8), :] = ro[cell, p, pl.ds(8, 8), :] + jnp.where(low, 0.0, change)
    rest, x3, y1, x2, y3 = condensed()
    for p in range(5):
        for h, rows in enumerate(swap_halves(rest[p], x3[p])):
            for end in range(2):
                send_r[pl.ds((28 * end + h) * R + p, 2, stride=2 * R), :] = rows[14 * end : 14 * end + 2]

    def outer(t):
        @pl.when(t != me)
        def _():
            send_to(send_r, recv_r, 1, t)

    for dy in (2, 1, 3, 0):
        for dc in (1, 0):
            outer(along_y[dy] + cores[dc])
    own_copy(send_r, recv_r, 1).start()

    def get(recv, row, e):
        return swap_halves(*(recv[pl.ds((2 * b + e) * R + row, 8, stride=4 * R), :] for b in range(2)))

    arrived(send_m, recv_m, 0)
    for e in range(2):
        for c in range(2):
            both = [get(recv_m, 2 * p + c, e) for p in range(5)]
            for side in range(2):
                u, v, w, h, sigma = (both[p][side] for p in range(5))
                k = 0.5 * (u * u + v * v + w * w)
                cell = 4 * e + c + 2 * side
                values = (u, v, w, h, k, sigma, 1.0 / (1.0 + 2.0 * sigma))
                for p in range(7):
                    prm[p, cell + 2] = values[p]
                    if cell >= 6:
                        prm[p, cell - 6] = previous(values[p], 1)
                    if cell == 0:
                        prm[p, 10] = following(values[p], 1)

    def gas(place_):
        return tuple(prm[p, place_] for p in range(5))

    def level_1(i, carry):
        at = 2 * i + 2
        sigma, before, after = prm[5, at], prm[5, at - 1], prm[5, at + 1]
        left = scaled(jacobian_rows(*gas(at - 1)), sigma, prm[6, at - 1])
        right = scaled(jacobian_rows(*gas(at + 1)), -sigma, prm[6, at + 1])
        here, far_left, far_right = gas(at), gas(at - 2), gas(at + 2)
        own = diagonal_rows(left, right, here, before, sigma, after)
        for r in range(5):
            lower = row_times_jacobian(left[r], far_left, before)
            upper = row_times_jacobian(right[r], far_right, -after)
            for c in range(5):
                d1[i + 1, r, c] = own[r][c]
                l1[i + 1, r, c] = -lower[c]
                l1[i + 1, r, 5 + c] = -upper[c]
        return carry

    for i in range(4):
        level_1(i, 0)

    def level_2_normalise(i, carry):
        normalise(d1, l1, 2 * i + 2, keep=False)
        return carry

    for i in range(2):
        level_2_normalise(i, 0)
    for r in range(5):
        l1[0, r] = previous(l1[4, r], 1)

    def rows_of(ref, s):
        return [ref[s, r] for r in range(5)]

    def level_2_combine(i, carry):
        s = 2 * i + 1
        combine(rows_of(l1, s), rows_of(d1, s), rows_of(l1, s - 1), rows_of(l1, s + 1), d2, l2, i)
        return carry

    for i in range(2):
        level_2_combine(i, 0)

    inverse_4, own_4 = normalised(rows_of(d2, 1), rows_of(l2, 1))
    own_0 = rows_of(l2, 0)
    diagonal, own = combined(own_0, rows_of(d2, 0), [previous(row, 1) for row in own_4], own_4)

    unit = identity(jnp.ones((8, 128), jnp.float32))
    levels = []
    for step in range(3):
        inverse, own = normalised(diagonal, own)
        levels.append((inverse, own))
        diagonal, own = combined(
            own, unit, [previous(x, 2**step) for x in own], [following(x, 2**step) for x in own]
        )
    q, _ = place((5, 8, 128))
    other = [jnp.where(q < 4, own[r][5:], own[r][:5]) for r in range(5)]
    both = solve_rows(*factor_rows(diagonal), [jnp.concatenate([other[r], unit[r]], axis=0) for r in range(5)])
    other, fourth = [row[:5] for row in both], [row[5:] for row in both]
    facing = [roll_rows(x, 4) for x in other]
    last = inverse_of([unit[r] - row_times(other[r], facing) for r in range(5)])

    arrived(send_r, recv_r, 1)
    parts = [[get(recv_r, p, e) for p in range(5)] for e in range(2)]
    inside = [[parts[e][p][1] for p in range(5)] for e in range(2)]
    four = {}
    for i, before in ((0, [previous(value, 1) for value in inside[1]]), (4, inside[0])):
        t = shifted(gas(i + 1), before, prm[5, i + 2])
        four[i] = [parts[i // 4][p][0] + t[p] for p in range(5)]
    y = {}
    y[4] = times(inverse_4, four[4])
    before = [previous(value, 1) for value in y[4]]
    b = [subtract(own_0[r], four[0][r], before, y[4]) for r in range(5)]
    for step in range(3):
        b = times(levels[step][0], b)
        before = [previous(value, 2**step) for value in b]
        after = [following(value, 2**step) for value in b]
        b = [subtract(levels[step][1][r], b[r], before, after) for r in range(5)]
    b = times(fourth, b)
    paired = [roll_rows(value, 4) for value in b]
    b = [b[r] - row_times(other[r], paired) for r in range(5)]
    x = {0: times(last, b)}
    x[8] = [following(value, 1) for value in x[0]]
    x[4] = [subtract(own_4[r], y[4][r], x[0], x[8]) for r in range(5)]

    for e in range(2):
        beyond = shifted(gas(4 * e + 6), x[4 * e + 4], -prm[5, 4 * e + 5])
        for p in range(5):
            for b, rows in enumerate(swap_halves(x[4 * e][p], beyond[p])):
                send_x[pl.ds((2 * b + e) * R + p, 8, stride=4 * R), :] = rows
    exchange(send_x, recv_x, 2)
    arrived(send_x, recv_x, 2)
    both = [swap_halves(*(recv_x[pl.ds(h * R + p, 16, stride=2 * R), :] for h in range(2))) for p in range(5)]
    x0 = [both[p][0] for p in range(5)]
    after = [inv3 * both[p][1] for p in range(5)]
    before = [inv1 * value for value in shifted(gas_own[0], x0, sig[1])]
    t = times(own_inverse, to_cell_2(before, [-value for value in after]))
    x2 = [x2[p] + t[p] for p in range(5)]
    x1, x3 = around([y1[p] + before[p] for p in range(5)], x2, [y3[p] - after[p] for p in range(5)])
    for p in range(5):
        out_ref[p, 0], out_ref[p, 1], out_ref[p, 2], out_ref[p, 3] = x0[p], x1[p], x2[p], x3[p]

    pl.when(has_up)(upward.wait_send)
    pl.when(has_down)(downward.wait_send)
    for which, (send, recv) in enumerate(((send_m, recv_m), (send_r, recv_r), (send_x, recv_x))):
        all_of(send, recv, which).wait_send()


def on_device(state, viscosity, residual_other):
    f32 = jnp.float32
    tile = (8, 128)
    buffer = pltpu.VMEM((N * R, 128), f32)
    return pl.pallas_call(
        kernel,
        out_shape=jax.ShapeDtypeStruct(state.shape, f32),
        in_specs=[pl.BlockSpec(memory_space=pltpu.HBM)] * 3,
        out_specs=pl.BlockSpec(memory_space=pltpu.VMEM),
        scratch_shapes=[
            pltpu.VMEM((5, 4, 32, 128), f32),
            pltpu.VMEM((4, 16, 128), f32),
            pltpu.VMEM((5, 4, 16, 128), f32),
            pltpu.VMEM((4, 5, 16, 128), f32),
            pltpu.VMEM((3, 5, 4, 2, 128), f32),
            pltpu.VMEM((3, 5, 4, 2, 128), f32),
            pltpu.VMEM((5, 32, 128), f32),
        ]
        + [buffer, buffer, pltpu.VMEM((3 * N * R // 2, 128), f32), buffer, buffer, buffer]
        + [
            pltpu.VMEM((7, 11) + tile, f32),
            pltpu.VMEM((5, 5, 5) + tile, f32),
            pltpu.VMEM((5, 5, 10) + tile, f32),
            pltpu.VMEM((2, 5, 5) + tile, f32),
            pltpu.VMEM((2, 5, 10) + tile, f32),
            pltpu.SemaphoreType.DMA((3,)),
            pltpu.SemaphoreType.DMA((2,)),
            pltpu.SemaphoreType.DMA((2,)),
            pltpu.SemaphoreType.DMA((3,)),
            pltpu.SemaphoreType.DMA((3,)),
            pltpu.SemaphoreType.DMA((3,)),
        ],
        compiler_params=pltpu.CompilerParams(
            collective_id=0, has_side_effects=True, vmem_limit_bytes=32 * 1024 * 1024
        ),
    )(*(pltpu.with_memory_space_constraint(x, pltpu.HBM) for x in (state, viscosity, residual_other)))


def solution(mesh):
    placed = (
        P(None, "stream", "normal", None),
        P("stream", "normal", None),
        P(None, "stream", "normal", None),
    )
    return jax.shard_map(
        on_device,
        mesh=mesh,
        in_specs=placed,
        out_specs=P(None, "stream", "normal", None),
        check_vma=False,
    )
```

```python
import jax
import jax.numpy as jnp
from jax import lax
from jax.experimental import pallas as pl
from jax.experimental.pallas import tpu as pltpu
from jax.sharding import PartitionSpec as P

N = 32
R = 16
ROWS = (10, 5, 5)
HALF = 64
MESH = pl.DeviceIdType.MESH


def roll_lanes(x):
    return pltpu.roll(x, HALF, axis=x.ndim - 1)


def roll_rows(x, by):
    return pltpu.roll(x, by % 8, axis=x.ndim - 2)


def swap_halves(a, b):
    low = lax.broadcasted_iota(jnp.int32, a.shape, a.ndim - 1) < HALF
    return jnp.where(low, a, roll_lanes(b)), jnp.where(low, roll_lanes(a), b)


def place(shape):
    q = lax.broadcasted_iota(jnp.int32, shape, len(shape) - 2)
    b = lax.broadcasted_iota(jnp.int32, shape, len(shape) - 1) >= HALF
    return q, b


def previous(x, by):
    q, b = place(x.shape)
    if by == 1:
        other = roll_lanes(x)
        return jnp.where(b, other, jnp.where(q == 0, 0.0, roll_rows(other, 1)))
    return jnp.where(q < by // 2, 0.0, roll_rows(x, by // 2))


def following(x, by):
    q, b = place(x.shape)
    if by == 1:
        other = roll_lanes(x)
        return jnp.where(b, jnp.where(q == 7, 0.0, roll_rows(other, -1)), other)
    return jnp.where(q >= 8 - by // 2, 0.0, roll_rows(x, -(by // 2)))


def jacobian_rows(u, v, w, h, k):
    return [
        [None, 1.0, None, None, None],
        [0.4 * k - u * u, 1.6 * u, -0.4 * v, -0.4 * w, 0.4],
        [-u * v, v, u, None, None],
        [-u * w, w, None, u, None],
        [u * (0.4 * k - h), h - 0.4 * u * u, -0.4 * u * v, -0.4 * u * w, 1.4 * u],
    ]


def jacobian_times(prm, m):
    u, v, w, h, k = prm
    t = m[1] - u * m[0]
    p = 0.4 * (k * m[0] - u * m[1] - v * m[2] - w * m[3] + m[4])
    return [
        m[1],
        p + u * (m[1] + t),
        v * t + u * m[2],
        w * t + u * m[3],
        u * (p + m[4]) + h * t,
    ]


def row_times_jacobian(g, prm, shift):
    u, v, w, h, k = prm
    e = g[0]
    for value, factor in ((g[1], u), (g[2], v), (g[3], w), (g[4], h)):
        if value is not None:
            e = value * factor if e is None else e + value * factor
    p = g[1] if g[4] is None else g[1] + u * g[4]
    p = 0.4 * p
    s = u + shift

    def part(index, other):
        return other if g[index] is None else s * g[index] + other

    return [
        part(0, k * p - u * e),
        part(1, e - u * p),
        part(2, -(v * p)),
        part(3, -(w * p)),
        part(4, p),
    ]


def scaled(rows, shift, factor):
    out = []
    for r in range(5):
        row = []
        for c in range(5):
            value = rows[r][c]
            if r == c:
                value = shift if value is None else value + shift
            row.append(None if value is None else value * factor)
        out.append(row)
    return out


def plus(a, b):
    if a is None:
        return b
    return a if b is None else a + b


def shifted(prm, m, shift):
    return [a + shift * b for a, b in zip(jacobian_times(prm, m), m)]


def diagonal_rows(left, right, here, before, sigma, after):
    rows = []
    for r in range(5):
        own = row_times_jacobian([plus(left[r][c], right[r][c]) for c in range(5)], here, 0.0)
        for c in range(5):
            if left[r][c] is not None:
                own[c] = own[c] + (after * right[r][c] - before * left[r][c])
        own[r] = own[r] + (1.0 + 2.0 * sigma)
        rows.append(own)
    return rows


def factor_rows(rows):
    rows = list(rows)
    recip = []
    for p in range(5):
        rec = 1.0 / rows[p][p]
        recip.append(rec)
        for r in range(p + 1, 5):
            weight = rows[r][p] * rec
            tail = rows[r][p + 1 :] - weight[None] * rows[p][p + 1 :] if p < 4 else None
            parts = [rows[r][:p], weight[None], tail] if p else [weight[None], tail]
            rows[r] = jnp.concatenate(parts, axis=0)
    return rows, recip


def solve_rows(lu, recip, right):
    x = list(right)
    for p in range(5):
        for r in range(p + 1, 5):
            x[r] = x[r] - lu[r][p] * x[p]
    for p in range(4, -1, -1):
        x[p] = x[p] * recip[p]
        for r in range(p):
            x[r] = x[r] - lu[r][p] * x[p]
    return x


def identity(like):
    one, zero = jnp.ones_like(like), jnp.zeros_like(like)
    return [jnp.stack([one if r == c else zero for c in range(5)]) for r in range(5)]


def inverse_of(rows):
    return solve_rows(*factor_rows(rows), identity(rows[0][0]))


def normalise(d_ref, x_ref, s, keep=True):
    rows = [d_ref[s, r] for r in range(5)]
    unit = identity(rows[0][0])
    right = [jnp.concatenate([x_ref[s, r], unit[r]], axis=0) if keep else x_ref[s, r] for r in range(5)]
    x = solve_rows(*factor_rows(rows), right)
    for r in range(5):
        x_ref[s, r] = x[r][:10]
        if keep:
            d_ref[s, r] = x[r][10:]


def times(rows, m):
    return [row_times(row, m) for row in rows]


def row_times(row, others):
    first = row[0] * others[0] + row[1] * others[1]
    return first + (row[2] * others[2] + row[3] * others[3]) + row[4] * others[4]


def combine(own, diagonal, before, after, d_ref, x_ref, s):
    for r in range(5):
        left = row_times(own[r][:5], before)
        right = row_times(own[r][5:], after)
        d_ref[s, r] = diagonal[r] - left[5:] - right[:5]
        x_ref[s, r] = jnp.concatenate([-left[:5], -right[5:]], axis=0)


def subtract(own, r, before, after):
    return r - (row_times(own[:5], before) + row_times(own[5:], after))


def kernel(
    state_ref, visc_ref, resid_ref, out_ref,
    st, vis, res, ro, halo, away, gg, send_m, recv_m, send_r, recv_r, send_x, recv_x,
    prm, d1, l1, d2, l2, dp, lp,
    in_sem, halo_send, halo_recv, a2a_send, a2a_recv, own_sem,
):
    me = lax.axis_index("stream")
    z = lax.axis_index("normal")
    z_count = lax.axis_size("normal")

    has_up, has_down = z < z_count - 1, z > 0
    along_x = [lax.rem(me // 8 + d, 4) * 8 for d in range(4)]
    along_y = [lax.rem(lax.rem(me // 2, 4) + d, 4) * 2 for d in range(4)]
    cores = [lax.rem(me, 2), 1 - lax.rem(me, 2)]
    steps = [(dx, dy, dc) for dx in range(4) for dy in range(4) for dc in (1, 0) if dx or dy or dc]
    steps.sort(key=lambda d: -(min(d[0], 4 - d[0]) + min(d[1], 4 - d[1])))

    def for_partners(action, first=0, last=N):
        for dx, dy, dc in steps[first:last]:
            action(along_x[dx] + along_y[dy] + cores[dc])

    barrier = pltpu.get_barrier_semaphore()

    def greet(t):
        pl.semaphore_signal(barrier, inc=1, device_id={"stream": t}, device_id_type=MESH)

    for_partners(greet, 0, 10)
    def load(k, source, target):
        return pltpu.make_async_copy(source, target, in_sem.at[k])

    loads = [
        load(0, state_ref, st.at[:, :, pl.ds(8, 16), :]),
        load(1, visc_ref, vis),
        load(2, resid_ref, res),
    ]
    for each in loads:
        each.start()

    halo[pl.ds(0, 2)] = jnp.zeros((2, 5, 4, 2, 128), jnp.float32)
    @pl.when(has_up)
    def _():
        pl.semaphore_signal(barrier, inc=1, device_id={"normal": z + 1}, device_id_type=MESH)

    @pl.when(has_down)
    def _():
        pl.semaphore_signal(barrier, inc=1, device_id={"normal": z - 1}, device_id_type=MESH)

    for_partners(greet, 10)
    for ends in (pl.ds(0, 8), pl.ds(24, 8)):
        st[:, :, ends, :] = jnp.zeros((5, 4, 8, 128), jnp.float32)
        gg[:, ends, :] = jnp.zeros((5, 8, 128), jnp.float32)

    slot = lax.rem(me + N - 4, N)

    def message(buf, which, t):
        return buf.at[pl.ds(pl.multiple_of(t * R, R), ROWS[which])]

    def slot_of(t):
        return lax.rem(t + N - 4, N)

    def there(send, recv, which, t):
        if which == 2:
            return message(send, which, t), message(recv, which, slot)
        return message(send, which, slot_of(t)), message(recv, which, me)

    def own_copy(send, recv, which):
        return pltpu.make_async_copy(*there(send, recv, which, me), own_sem.at[which])

    def send_to(send, recv, which, t):
        source, target = there(send, recv, which, t)
        pltpu.make_async_remote_copy(
            src_ref=source, dst_ref=target,
            send_sem=a2a_send.at[which], recv_sem=a2a_recv.at[which],
            device_id={"stream": t}, device_id_type=MESH,
        ).start()

    def exchange(send, recv, which):
        for_partners(lambda t: send_to(send, recv, which, t))
        own_copy(send, recv, which).start()

    def all_of(send, recv, which):
        return pltpu.make_async_remote_copy(
            src_ref=send.at[pl.ds(0, (N - 1) * ROWS[which])], dst_ref=recv.at[pl.ds(0, (N - 1) * ROWS[which])],
            send_sem=a2a_send.at[which], recv_sem=a2a_recv.at[which],
            device_id={"stream": lax.rem(me + 1, N)}, device_id_type=MESH,
        )

    def arrived(send, recv, which):
        all_of(send, recv, which).wait_recv()
        own_copy(send, recv, which).wait()

    def put(send, row, a, b):
        for h, rows in enumerate(swap_halves(a, b)):
            send[pl.ds(h * R + row, 16, stride=2 * R), :] = rows

    loads[0].wait()
    loads[1].wait()
    for p in range(5):
        for cell in range(4):
            away[0, p, cell] = st[p, cell, pl.ds(22, 2), :]
            away[1, p, cell] = st[p, cell, pl.ds(8, 2), :]
    gas_own, sig = [], [vis[cell] for cell in range(4)]
    for cell in range(4):
        rho, m1, m2, m3, energy = (st[p, cell, pl.ds(8, 16), :] for p in range(5))
        inverse = 1.0 / rho
        u, v, w = m1 * inverse, m2 * inverse, m3 * inverse
        k = 0.5 * (u * u + v * v + w * w)
        gas_own.append((u, v, w, 1.4 * energy * inverse - 0.4 * k, k))
    for c in range(2):
        for p in range(4):
            put(send_m, 2 * p + c, gas_own[c][p], gas_own[c + 2][p])
        put(send_m, 8 + c, sig[c], sig[c + 2])

    def flux_of(q):
        rho, m1, m2, m3, energy = q
        inverse = 1.0 / rho
        pressure = 0.4 * (energy - 0.5 * (m1 * m1 + m2 * m2 + m3 * m3) * inverse)
        v = m2 * inverse
        return [m2, m1 * v, m2 * v + pressure, m3 * v, (energy + pressure) * v]

    loads[2].wait()
    for cell in range(4):
        flux = flux_of([st[p, cell, pl.ds(8, 16), :] for p in range(5)])
        for p in range(5):
            gg[p, pl.ds(8, 16)] = flux[p]
            s = {d: st[p, cell, pl.ds(8 + d, 16), :] for d in (-2, -1, 0, 1, 2)}
            g = {d: gg[p, pl.ds(8 + d, 16), :] for d in (-1, 1)}
            ro[cell, p] = (
                res[p, cell]
                - 40.0 * (g[1] - g[-1])
                + vis[cell] * (s[1] - 2.0 * s[0] + s[-1])
                - 8.0 * (s[2] - 4.0 * s[1] + 6.0 * s[0] - 4.0 * s[-1] + s[-2])
            )

    inv1, inv3 = (1.0 / (1.0 + 2.0 * sig[cell]) for cell in (1, 3))
    own_inverse = inverse_of([
        jnp.stack(values)
        for values in diagonal_rows(
            scaled(jacobian_rows(*gas_own[1]), sig[2], inv1), scaled(jacobian_rows(*gas_own[3]), -sig[2], inv3),
            gas_own[2], sig[1], sig[2], sig[3],
        )
    ])

    def around(y1, x2, y3):
        flux = jacobian_times(gas_own[2], x2)
        x1 = [y1[p] - inv1 * (flux[p] - sig[1] * x2[p]) for p in range(5)]
        return x1, [y3[p] + inv3 * (flux[p] + sig[3] * x2[p]) for p in range(5)]

    def to_cell_2(y1, y3):
        a, b = shifted(gas_own[1], y1, sig[2]), shifted(gas_own[3], y3, -sig[2])
        return [a[p] - b[p] for p in range(5)]

    def condensed():
        y1, y3 = [inv1 * ro[1, p] for p in range(5)], [inv3 * ro[3, p] for p in range(5)]
        t = to_cell_2(y1, y3)
        x2 = times(own_inverse, [ro[2, p] + t[p] for p in range(5)])
        x1, x3 = around(y1, x2, y3)
        t = shifted(gas_own[1], x1, -sig[0])
        return [ro[0, p] - t[p] for p in range(5)], x3, y1, x2, y3

    rest, x3, *_ = condensed()
    for p in range(5):
        put(send_r, p, rest[p], x3[p])

    pl.semaphore_wait(barrier, N - 1 + has_up.astype(jnp.int32) + has_down.astype(jnp.int32))
    upward = pltpu.make_async_remote_copy(
        src_ref=away.at[0], dst_ref=halo.at[0],
        send_sem=halo_send.at[0], recv_sem=halo_recv.at[0],
        device_id={"normal": lax.rem(z + 1, z_count)}, device_id_type=MESH,
    )
    downward = pltpu.make_async_remote_copy(
        src_ref=away.at[1], dst_ref=halo.at[1],
        send_sem=halo_send.at[1], recv_sem=halo_recv.at[1],
        device_id={"normal": lax.rem(z + z_count - 1, z_count)}, device_id_type=MESH,
    )
    pl.when(has_up)(upward.start)
    pl.when(has_down)(downward.start)
    exchange(send_m, recv_m, 0)

    def inner(t):
        @pl.when(t >= 8)
        def _():
            send_to(send_r, recv_r, 1, t)

    for_partners(inner)

    pl.when(has_down)(upward.wait_recv)
    pl.when(has_up)(downward.wait_recv)
    index = lax.broadcasted_iota(jnp.int32, (8, 128), 0)
    low = index < 4
    edge = (index == 0) | (index == 7)

    def inward(plane):
        return jnp.where(low, roll_rows(plane, -1), roll_rows(plane, 1))

    for cell in range(4):
        between = jnp.zeros((4, 128), jnp.float32)
        q = [jnp.concatenate([halo[0, p, cell], between, halo[1, p, cell]], axis=0) for p in range(5)]
        flux = flux_of([jnp.where(q[0] > 0.0, q[0], 1.0)] + q[1:])
        factor = 32.0 + jnp.where(low, vis[cell, pl.ds(0, 8), :], vis[cell, pl.ds(8, 8), :])
        for p in range(5):
            change = jnp.where(edge, factor * inward(q[p]) + jnp.where(low, 40.0, -40.0) * inward(flux[p]), 0.0)
            change = change - 8.0 * q[p]
            ro[cell, p, pl.ds(0, 8), :] = ro[cell, p, pl.ds(0, 8), :] + jnp.where(low, change, 0.0)
            ro[cell, p, pl.ds(8, 8), :] = ro[cell, p, pl.ds(8, 8), :] + jnp.where(low, 0.0, change)
    rest, x3, y1, x2, y3 = condensed()
    for p in range(5):
        for h, rows in enumerate(swap_halves(rest[p], x3[p])):
            for end in range(2):
                send_r[pl.ds((28 * end + h) * R + p, 2, stride=2 * R), :] = rows[14 * end : 14 * end + 2]

    def outer(t):
        @pl.when(t != me)
        def _():
            send_to(send_r, recv_r, 1, t)

    for dy in (2, 1, 3, 0):
        for dc in (1, 0):
            outer(along_y[dy] + cores[dc])
    own_copy(send_r, recv_r, 1).start()

    def get(recv, row, e):
        return swap_halves(*(recv[pl.ds((2 * b + e) * R + row, 8, stride=4 * R), :] for b in range(2)))

    arrived(send_m, recv_m, 0)
    for e in range(2):
        for c in range(2):
            both = [get(recv_m, 2 * p + c, e) for p in range(5)]
            for side in range(2):
                u, v, w, h, sigma = (both[p][side] for p in range(5))
                k = 0.5 * (u * u + v * v + w * w)
                cell = 4 * e + c + 2 * side
                values = (u, v, w, h, k, sigma, 1.0 / (1.0 + 2.0 * sigma))
                for p in range(7):
                    prm[p, cell + 2] = values[p]
                    if cell >= 6:
                        prm[p, cell - 6] = previous(values[p], 1)
                    if cell == 0:
                        prm[p, 10] = following(values[p], 1)

    def gas(place_):
        return tuple(prm[p, place_] for p in range(5))

    def level_1(i, carry):
        at = 2 * i + 2
        sigma, before, after = prm[5, at], prm[5, at - 1], prm[5, at + 1]
        left = scaled(jacobian_rows(*gas(at - 1)), sigma, prm[6, at - 1])
        right = scaled(jacobian_rows(*gas(at + 1)), -sigma, prm[6, at + 1])
        here, far_left, far_right = gas(at), gas(at - 2), gas(at + 2)
        own = diagonal_rows(left, right, here, before, sigma, after)
        for r in range(5):
            lower = row_times_jacobian(left[r], far_left, before)
            upper = row_times_jacobian(right[r], far_right, -after)
            for c in range(5):
                d1[i + 1, r, c] = own[r][c]
                l1[i + 1, r, c] = -lower[c]
                l1[i + 1, r, 5 + c] = -upper[c]
        return carry

    for i in range(4):
        level_1(i, 0)

    def level_2_normalise(i, carry):
        normalise(d1, l1, 2 * i + 2, keep=False)
        return carry

    for i in range(2):
        level_2_normalise(i, 0)
    for r in range(5):
        l1[0, r] = previous(l1[4, r], 1)

    def rows_of(ref, s):
        return [ref[s, r] for r in range(5)]

    def level_2_combine(i, carry):
        s = 2 * i + 1
        combine(rows_of(l1, s), rows_of(d1, s), rows_of(l1, s - 1), rows_of(l1, s + 1), d2, l2, i)
        return carry

    for i in range(2):
        level_2_combine(i, 0)

    normalise(d2, l2, 1)
    combine(
        rows_of(l2, 0), rows_of(d2, 0), [previous(l2[1, r], 1) for r in range(5)], rows_of(l2, 1), dp, lp, 0
    )

    unit = identity(jnp.ones((8, 128), jnp.float32))
    for step in range(3):
        normalise(dp, lp, step)
        own = rows_of(lp, step)
        combine(
            own, unit, [previous(x, 2**step) for x in own], [following(x, 2**step) for x in own],
            dp, lp, step + 1,
        )
    q, _ = place((5, 8, 128))
    other = [jnp.where(q < 4, lp[3, r, pl.ds(5, 5)], lp[3, r, pl.ds(0, 5)]) for r in range(5)]
    both = solve_rows(*factor_rows(rows_of(dp, 3)), [jnp.concatenate([other[r], unit[r]], axis=0) for r in range(5)])
    other, fourth = [row[:5] for row in both], [row[5:] for row in both]
    facing = [roll_rows(x, 4) for x in other]
    last = inverse_of([unit[r] - row_times(other[r], facing) for r in range(5)])

    arrived(send_r, recv_r, 1)
    parts = [[get(recv_r, p, e) for p in range(5)] for e in range(2)]
    inside = [[parts[e][p][1] for p in range(5)] for e in range(2)]
    four = {}
    for i, before in ((0, [previous(value, 1) for value in inside[1]]), (4, inside[0])):
        t = shifted(gas(i + 1), before, prm[5, i + 2])
        four[i] = [parts[i // 4][p][0] + t[p] for p in range(5)]
    y = {}
    y[4] = times(rows_of(d2, 1), four[4])
    before = [previous(value, 1) for value in y[4]]
    b = [subtract(l2[0, r], four[0][r], before, y[4]) for r in range(5)]
    for step in range(3):
        b = times(rows_of(dp, step), b)
        before = [previous(value, 2**step) for value in b]
        after = [following(value, 2**step) for value in b]
        b = [subtract(lp[step, r], b[r], before, after) for r in range(5)]
    b = times(fourth, b)
    paired = [roll_rows(value, 4) for value in b]
    b = [b[r] - row_times(other[r], paired) for r in range(5)]
    x = {0: times(last, b)}
    x[8] = [following(value, 1) for value in x[0]]
    x[4] = [subtract(l2[1, r], y[4][r], x[0], x[8]) for r in range(5)]

    for e in range(2):
        beyond = shifted(gas(4 * e + 6), x[4 * e + 4], -prm[5, 4 * e + 5])
        for p in range(5):
            for b, rows in enumerate(swap_halves(x[4 * e][p], beyond[p])):
                send_x[pl.ds((2 * b + e) * R + p, 8, stride=4 * R), :] = rows
    exchange(send_x, recv_x, 2)
    arrived(send_x, recv_x, 2)
    both = [swap_halves(*(recv_x[pl.ds(h * R + p, 16, stride=2 * R), :] for h in range(2))) for p in range(5)]
    x0 = [both[p][0] for p in range(5)]
    after = [inv3 * both[p][1] for p in range(5)]
    before = [inv1 * value for value in shifted(gas_own[0], x0, sig[1])]
    t = times(own_inverse, to_cell_2(before, [-value for value in after]))
    x2 = [x2[p] + t[p] for p in range(5)]
    x1, x3 = around([y1[p] + before[p] for p in range(5)], x2, [y3[p] - after[p] for p in range(5)])
    for p in range(5):
        out_ref[p, 0], out_ref[p, 1], out_ref[p, 2], out_ref[p, 3] = x0[p], x1[p], x2[p], x3[p]

    pl.when(has_up)(upward.wait_send)
    pl.when(has_down)(downward.wait_send)
    for which, (send, recv) in enumerate(((send_m, recv_m), (send_r, recv_r), (send_x, recv_x))):
        all_of(send, recv, which).wait_send()


def on_device(state, viscosity, residual_other):
    f32 = jnp.float32
    tile = (8, 128)
    buffer = pltpu.VMEM((N * R, 128), f32)
    return pl.pallas_call(
        kernel,
        out_shape=jax.ShapeDtypeStruct(state.shape, f32),
        in_specs=[pl.BlockSpec(memory_space=pltpu.HBM)] * 3,
        out_specs=pl.BlockSpec(memory_space=pltpu.VMEM),
        scratch_shapes=[
            pltpu.VMEM((5, 4, 32, 128), f32),
            pltpu.VMEM((4, 16, 128), f32),
            pltpu.VMEM((5, 4, 16, 128), f32),
            pltpu.VMEM((4, 5, 16, 128), f32),
            pltpu.VMEM((3, 5, 4, 2, 128), f32),
            pltpu.VMEM((3, 5, 4, 2, 128), f32),
            pltpu.VMEM((5, 32, 128), f32),
        ]
        + [buffer, buffer, pltpu.VMEM((3 * N * R // 2, 128), f32), buffer, buffer, buffer]
        + [
            pltpu.VMEM((7, 11) + tile, f32),
            pltpu.VMEM((5, 5, 5) + tile, f32),
            pltpu.VMEM((5, 5, 10) + tile, f32),
            pltpu.VMEM((2, 5, 5) + tile, f32),
            pltpu.VMEM((2, 5, 10) + tile, f32),
            pltpu.VMEM((4, 5, 5) + tile, f32),
            pltpu.VMEM((4, 5, 10) + tile, f32),
            pltpu.SemaphoreType.DMA((3,)),
            pltpu.SemaphoreType.DMA((2,)),
            pltpu.SemaphoreType.DMA((2,)),
            pltpu.SemaphoreType.DMA((3,)),
            pltpu.SemaphoreType.DMA((3,)),
            pltpu.SemaphoreType.DMA((3,)),
        ],
        compiler_params=pltpu.CompilerParams(
            collective_id=0, has_side_effects=True, vmem_limit_bytes=32 * 1024 * 1024
        ),
    )(*(pltpu.with_memory_space_constraint(x, pltpu.HBM) for x in (state, viscosity, residual_other)))


def solution(mesh):
    placed = (
        P(None, "stream", "normal", None),
        P("stream", "normal", None),
        P(None, "stream", "normal", None),
    )
    return jax.shard_map(
        on_device,
        mesh=mesh,
        in_specs=placed,
        out_specs=P(None, "stream", "normal", None),
        check_vma=False,
    )
```
